32 devices in a mesh: grp: 2 (over x), pole: 4 (over z), row: 4 (over y, core).
Axes of the slice: x: 2, y: 2, z: 4, core: 2. Of those that a mesh axis runs over, the one named last changes fastest.
Arguments:
- aux_modes: float32 [64, 2, 3072, 128], P(('grp', 'pole'), None, 'row'), parts along dimension 0, may hold values from -6 to 6
- rho_panel: float32 [2, 6144, 256], P(None, ('grp', 'row')), parts along dimension 1, may hold values from -6 to 6
- ham_blocks: float32 [48, 5, 2, 128, 128], P(('grp', 'row')), parts along dimension 0, may hold values from -0.25 to 0.25
- block_counts: int32 [48], P(('grp', 'row')), parts along dimension 0, may hold values from 1 to 5, as said below
- block_offsets: int32 [48, 5], P(('grp', 'row')), parts along dimension 0, may hold values from -2 to 2, as said below
- lead_gamma: float32 [2, 2, 128, 128], replicated, may hold values from -0.5 to 0.5
- pole_energy: float32 [2, 64], P(None, ('grp', 'pole')), parts along dimension 1, may hold values from -1 to 1
- residues: float32 [2, 64], P(None, ('grp', 'pole')), parts along dimension 1, may hold values from -1.2 to 1.2
- pole_lead: int32 [64], P(('grp', 'pole')), parts along dimension 0, may hold values from 0 to 1, as said below
Outputs:
- slopes: float32 [64, 2, 3072, 128], P(('grp', 'pole'), None, 'row'), parts along dimension 0
- lead_term: float32 [2, 6144, 256], P(None, ('grp', 'row')), parts along dimension 1
The draws below stay inside these ranges and needn't reach their ends.
There are 2 independent parts, one for each index of `grp`. The reference program is written for one: setup_inputs(seed, part) draws one part's arguments, and reference() takes and returns one part's arrays. A program takes and returns all parts, laid end to end along the dimension named above; an argument that names none is the same for every part. Nothing has to cross between parts.
Inputs may be any that keep to these rules, and one draw needn't show every extreme that they name: `block_counts`: some row block uses all 5 slots and some only one. `block_offsets`: slot 0 of every row block is 0; the 5 entries of a row block are distinct. `pole_lead`: each lead has exactly 16 poles.
All inputs are finite; a program needn't handle non-finite values.
Results may differ from the reference program's by a relative error of at most 0.0003.
Values sent between devices are 32-bit elements; how exact they have to be, the bound alone decides.
No kernel may reach another device: no remote copies, remote signals or barrier semaphores. Data moves between devices by JAX's collectives and lax.ppermute only.
A program may use at most 128 MiB of HBM per device.

```python
import jax
import jax.numpy as jnp
from jax import lax

NC = 128
BLK = 128
REACH = 2
KMAX = 5
POLES = 32
BLK_DEV = 6
NBLOCKS = 24
NORB = 3072


def draw_block_counts(key, part):
    key = jax.random.fold_in(key, 11)
    first_key, second_key, third_key, fourth_key = jax.random.split(key, 4)
    groups = NBLOCKS // BLK_DEV
    levels = jax.random.randint(first_key, (groups,), 1, KMAX + 1)
    levels = jnp.repeat(levels, BLK_DEV)
    counts = jax.random.randint(second_key, (NBLOCKS,), 0, 1 << 20) % levels + 1
    top_pos = jax.random.randint(third_key, (), 0, NBLOCKS)
    low_pos = (top_pos + 1 + jax.random.randint(fourth_key, (), 0, NBLOCKS - 1)) % NBLOCKS
    positions = jnp.arange(NBLOCKS)
    counts = jnp.where(positions == top_pos, KMAX, counts)
    counts = jnp.where(positions == low_pos, 1, counts)
    return counts.astype(jnp.int32)


def draw_block_offsets(key, part):
    key = jax.random.fold_in(key, 23)
    row_keys = jax.random.split(key, NBLOCKS)
    side_offsets = jnp.concatenate([jnp.arange(-REACH, 0), jnp.arange(1, REACH + 1)]).astype(jnp.int32)
    shuffled = jax.vmap(lambda row_key: jax.random.permutation(row_key, side_offsets))(row_keys)
    return jnp.concatenate([jnp.zeros((NBLOCKS, 1), jnp.int32), shuffled], axis=1).astype(jnp.int32)


def draw_pole_lead(key, part):
    key = jax.random.fold_in(key, 37)
    shuffled = jax.random.permutation(key, POLES)
    return (shuffled % 2).astype(jnp.int32)


def block_levels(key, dims, cuts, smallest, largest):
    level = 1.0
    for position, parts in cuts:
        heights = jax.random.uniform(jax.random.fold_in(jax.random.fold_in(key, 6), position), (parts,), jnp.float32, smallest / len(cuts), largest / len(cuts))
        level = level * jnp.repeat(jnp.exp(heights), dims[position] // parts).reshape((-1,) + (1,) * (len(dims) - 1 - position))
    return level


def gaussian(stream_key, dims, scale, limit, pieces=(), kind=jnp.bfloat16):
    entries = jax.random.normal(stream_key, dims, jnp.float32) * scale
    if len(pieces) > 0:
        entries = block_levels(stream_key, dims, pieces, -0.22, 0.18) * entries
    return jnp.clip(entries, min=-limit, max=limit).astype(kind)


def setup_inputs(seed: int = 0, part: int = 0) -> dict:
    key_of = jax.random.split(jax.random.key(seed), 10)
    part_keys = jax.random.split(jax.random.fold_in(key_of[9], part), 10)
    aux_modes = gaussian(part_keys[0], (POLES, 2, NORB, NC), 1.0, 6.0, ((0, 4), (2, 4)), jnp.float32)
    rho_panel = gaussian(part_keys[1], (2, NORB, 2 * NC), 1.0, 6.0, ((1, 4),), jnp.float32)
    ham_blocks = gaussian(part_keys[2], (NBLOCKS, KMAX, 2, BLK, BLK), (BLK * KMAX) ** -0.5, 0.25, ((0, 4),), jnp.float32)
    block_counts = draw_block_counts(jax.random.fold_in(jax.random.fold_in(key_of[9], part), 71), part)
    block_offsets = draw_block_offsets(jax.random.fold_in(jax.random.fold_in(key_of[9], part), 71), part)
    lead_gamma = gaussian(key_of[5], (2, 2, NC, NC), NC ** -0.5, 0.5, (), jnp.float32)
    pole_energy = jnp.clip(jax.random.uniform(part_keys[6], (2, POLES), jnp.float32, -1.0, 1.0) * block_levels(part_keys[6], (2, POLES), ((1, 4),), -0.4, 0.0), -1.0, 1.0)
    residues = gaussian(part_keys[7], (2, POLES), 0.2, 1.2, ((1, 4),), jnp.float32)
    pole_lead = draw_pole_lead(jax.random.fold_in(jax.random.fold_in(key_of[9], part), 71), part)
    return dict(aux_modes=aux_modes, rho_panel=rho_panel, ham_blocks=ham_blocks, block_counts=block_counts, block_offsets=block_offsets, lead_gamma=lead_gamma, pole_energy=pole_energy, residues=residues, pole_lead=pole_lead)


HIGH = lax.Precision.HIGHEST


def matmul_high(left, right):
    return jnp.dot(left, right, precision=HIGH)


def lead_mixing(aux_modes, residues, pole_lead):
    lead_mask = (pole_lead[:, None] == jnp.arange(2, dtype=jnp.int32)[None, :]).astype(aux_modes.dtype)
    coef_real = lead_mask * residues[0][:, None]
    coef_imag = lead_mask * residues[1][:, None]

    def mixing(coef, mode_field):
        summed = jnp.einsum("pa,prc->rac", coef, mode_field, precision=HIGH)
        return summed.reshape(mode_field.shape[1], -1)

    sum_real = mixing(coef_real, aux_modes[:, 0]) - mixing(coef_imag, aux_modes[:, 1])
    sum_imag = mixing(coef_real, aux_modes[:, 1]) + mixing(coef_imag, aux_modes[:, 0])
    return jnp.stack([sum_real, sum_imag])


def lead_source(section_value, lead_gamma):
    width = lead_gamma.shape[-1]
    real_list = []
    imag_list = []
    for lead_no in range(2):
        section_real = section_value[0, :, lead_no * width:(lead_no + 1) * width]
        section_imag = section_value[1, :, lead_no * width:(lead_no + 1) * width]
        gamma_pair = lead_gamma[lead_no]
        real_list.append(matmul_high(section_real, gamma_pair[0]) - matmul_high(section_imag, gamma_pair[1]))
        imag_list.append(matmul_high(section_real, gamma_pair[1]) + matmul_high(section_imag, gamma_pair[0]))
    return jnp.stack([jnp.stack(real_list), jnp.stack(imag_list)])


def slope_from(ham_image, mode_field, energy_real, energy_imag, pole_source):
    total_real = ham_image[..., 0, :, :] - (energy_real * mode_field[..., 0, :, :] - energy_imag * mode_field[..., 1, :, :]) + pole_source[..., 0, :, :]
    total_imag = ham_image[..., 1, :, :] - (energy_real * mode_field[..., 1, :, :] + energy_imag * mode_field[..., 0, :, :]) + pole_source[..., 1, :, :]
    return jnp.stack([total_imag, -total_real], axis=-3)


def apply_hamiltonian(mode_field, ham_blocks, block_counts, block_offsets):
    width = ham_blocks.shape[-1]
    columns = mode_field.shape[-1]
    padded = jnp.pad(mode_field, ((0, 0), (REACH * width, REACH * width), (0, 0)))
    blocks = padded.reshape(2, NBLOCKS + 2 * REACH, width, columns)
    row_ids = jnp.arange(NBLOCKS, dtype=jnp.int32)
    total = jnp.zeros((2, NBLOCKS, width, columns), mode_field.dtype)

    def batched(left, right):
        return jnp.einsum("rij,rjc->ric", left, right, precision=HIGH)

    for which in range(KMAX):
        picked = blocks[:, (row_ids + block_offsets[:, which] + REACH).astype(jnp.int32)]
        alive_mask = (which < block_counts).astype(mode_field.dtype)[:, None, None]
        ham_real = ham_blocks[:, which, 0]
        ham_imag = ham_blocks[:, which, 1]
        real_part = batched(ham_real, picked[0]) - batched(ham_imag, picked[1])
        imag_part = batched(ham_real, picked[1]) + batched(ham_imag, picked[0])
        total = total + alive_mask[None] * jnp.stack([real_part, imag_part])
    return total.reshape(2, NBLOCKS * width, columns)


def reference(aux_modes, rho_panel, ham_blocks, block_counts, block_offsets, lead_gamma, pole_energy, residues, pole_lead):
    lead_term = lead_mixing(aux_modes, residues, pole_lead)
    section_value = rho_panel + 0.25 * lead_term
    source = lead_source(section_value, lead_gamma)

    def one_pole(items):
        mode_field, energy, lead_id = items
        ham_image = apply_hamiltonian(mode_field, ham_blocks, block_counts, block_offsets)
        pole_source = jnp.where(lead_id == 0, source[:, 0], source[:, 1])
        return slope_from(ham_image, mode_field, energy[0], energy[1], pole_source)

    slopes = lax.map(one_pole, (aux_modes, pole_energy.T, pole_lead))
    return slopes, lead_term
```

```python
import functools

import jax
import jax.numpy as jnp
from jax import lax
from jax.experimental import pallas as pl
from jax.experimental.pallas import tpu as pltpu
from jax.sharding import PartitionSpec as P

REACH = 2
CHUNKS = 4
F32 = jnp.float32
BF16 = jnp.bfloat16
SMEM = pltpu.MemorySpace.SMEM


def split_high_low(value):
    high = value.astype(BF16)
    return high, (value - high.astype(F32)).astype(BF16)


def mix_kernel(lead_ref, residue_ref, aux_ref, out_ref):
    poles = aux_ref.shape[0]
    width = aux_ref.shape[-1]
    sums = [None] * 4
    for pole in range(poles):
        real = aux_ref[pole, 0]
        imag = aux_ref[pole, 1]
        for lead in range(2):
            alive = (lead_ref[pole] == lead).astype(F32)
            coef_real = alive * residue_ref[0, pole]
            coef_imag = alive * residue_ref[1, pole]
            term_real = coef_real * real - coef_imag * imag
            term_imag = coef_real * imag + coef_imag * real
            if pole == 0:
                sums[lead] = term_real
                sums[2 + lead] = term_imag
            else:
                sums[lead] = sums[lead] + term_real
                sums[2 + lead] = sums[2 + lead] + term_imag
    for lead in range(2):
        out_ref[0, :, lead * width : (lead + 1) * width] = sums[lead]
        out_ref[1, :, lead * width : (lead + 1) * width] = sums[2 + lead]


def mix_rows(aux_modes, pole_lead, residues, first, rows, step):
    poles, _, _, width = aux_modes.shape
    return pl.pallas_call(
        mix_kernel,
        grid=(rows // step,),
        in_specs=[
            pl.BlockSpec(memory_space=SMEM),
            pl.BlockSpec(memory_space=SMEM),
            pl.BlockSpec((poles, 2, step, width), lambda i: (0, 0, first // step + i, 0)),
        ],
        out_specs=pl.BlockSpec((2, step, 2 * width), lambda i: (0, i, 0)),
        out_shape=jax.ShapeDtypeStruct((2, rows, 2 * width), F32),
        cost_estimate=pl.CostEstimate(
            flops=32 * poles * rows * width,
            bytes_accessed=8 * poles * rows * width + 16 * rows * width,
            transcendentals=0,
        ),
        name="mix",
    )(pole_lead, residues, aux_modes)


def ham_kernel(
    count_ref, offset_ref, odd_ref, energy_ref,
    ham_ref, aux_ref, near_ref, far_ref,
    out_ref,
    high_ref, low_ref, total_ref,
):
    row = pl.program_id(0)
    poles, _, rows, width = aux_ref.shape
    nblock = rows // width

    def put(place, source_ref, start):
        for pole in range(poles):
            for part in range(2):
                high, low = split_high_low(source_ref[pole, part, pl.ds(start, width), :])
                where = (place, pl.ds(part * width, width), pl.ds(pole * width, width))
                high_ref[where] = high
                low_ref[where] = low

    @pl.when(row == 0)
    def _():
        for block in range(nblock):
            put(REACH + block, aux_ref, block * width)
        odd = odd_ref[0]
        near_place = jnp.where(odd == 1, 0, nblock + REACH)
        far_place = jnp.where(odd == 1, nblock + REACH, 0)
        for block in range(REACH):
            put(near_place + block, near_ref, block * width)
            put(far_place + block, far_ref, block * width)

    total_ref[...] = jnp.zeros_like(total_ref)

    def slot(which, carry):
        place = row + REACH + offset_ref[row, which]
        ham_real = ham_ref[0, which, 0]
        ham_imag = ham_ref[0, which, 1]
        pair = jnp.concatenate(
            [
                jnp.concatenate([ham_real, -ham_imag], axis=1),
                jnp.concatenate([ham_imag, ham_real], axis=1),
            ],
            axis=0,
        )
        pair_high, pair_low = split_high_low(pair)
        high = high_ref[place]
        low = low_ref[place]
        dot = functools.partial(jnp.dot, preferred_element_type=F32)
        total_ref[...] += dot(pair_high, high) + dot(pair_high, low) + dot(pair_low, high)
        return carry

    lax.fori_loop(0, count_ref[row], slot, 0)

    start = pl.multiple_of(row * width, width)
    for pole in range(poles):
        real = aux_ref[pole, 0, pl.ds(start, width), :]
        imag = aux_ref[pole, 1, pl.ds(start, width), :]
        energy_real = energy_ref[0, pole]
        energy_imag = energy_ref[1, pole]
        columns = slice(pole * width, (pole + 1) * width)
        out_ref[pole, 0] = total_ref[width:, columns] - (energy_real * imag + energy_imag * real)
        out_ref[pole, 1] = (energy_real * real - energy_imag * imag) - total_ref[:width, columns]


def ham_part(aux_modes, near, far, ham_blocks, block_counts, block_offsets, odd, pole_energy):
    poles, _, rows, width = aux_modes.shape
    nblock, slots = ham_blocks.shape[:2]
    smem = pl.BlockSpec(memory_space=SMEM)
    whole = lambda r: (0, 0, 0, 0)
    places = nblock + 2 * REACH
    return pl.pallas_call(
        ham_kernel,
        grid=(nblock,),
        in_specs=[
            smem,
            smem,
            smem,
            smem,
            pl.BlockSpec((1, slots, 2, width, width), lambda r: (r, 0, 0, 0, 0)),
            pl.BlockSpec(aux_modes.shape, whole),
            pl.BlockSpec(near.shape, whole),
            pl.BlockSpec(far.shape, whole),
        ],
        out_specs=pl.BlockSpec((poles, 2, width, width), lambda r: (0, 0, r, 0)),
        out_shape=jax.ShapeDtypeStruct(aux_modes.shape, F32),
        scratch_shapes=[
            pltpu.VMEM((places, 2 * width, poles * width), BF16),
            pltpu.VMEM((places, 2 * width, poles * width), BF16),
            pltpu.VMEM((2 * width, poles * width), F32),
        ],
        compiler_params=pltpu.CompilerParams(vmem_limit_bytes=56 * 2**20),
        cost_estimate=pl.CostEstimate(
            flops=6 * nblock * slots * (2 * width) ** 2 * poles * width,
            bytes_accessed=4 * (2 * aux_modes.size + near.size + far.size + ham_blocks.size),
            transcendentals=0,
        ),
        name="ham",
    )(block_counts, block_offsets, odd, pole_energy, ham_blocks, aux_modes, near, far)


def finish_kernel(
    lead_ref, taken_ref, gamma_ref, rho_ref, local_ref, received_ref, slope_ref, *rest
):
    out_ref, lead_out_ref, source_ref = rest[-3:]
    poles = slope_ref.shape[0]
    width = slope_ref.shape[-1]
    taken = taken_ref[0] == 1
    lead_term = jnp.where(taken, received_ref[...], local_ref[...])
    lead_out_ref[...] = lead_term
    section = rho_ref[...] + 0.25 * lead_term
    for lead in range(2):
        columns = slice(lead * width, (lead + 1) * width)
        pair = jnp.concatenate([section[0, :, columns], section[1, :, columns]], axis=1)
        gamma_real = gamma_ref[lead, 0]
        gamma_imag = gamma_ref[lead, 1]
        gamma = jnp.concatenate(
            [
                jnp.concatenate([gamma_real, gamma_imag], axis=1),
                jnp.concatenate([-gamma_imag, gamma_real], axis=1),
            ],
            axis=0,
        )
        pair_high, pair_low = split_high_low(pair)
        gamma_high, gamma_low = split_high_low(gamma)
        dot = functools.partial(jnp.dot, preferred_element_type=F32)
        source_ref[lead] = (
            dot(pair_high, gamma_high) + dot(pair_high, gamma_low) + dot(pair_low, gamma_high)
        )
    for pole in range(poles):
        lead = lead_ref[pole]
        out_ref[pole, 0] = slope_ref[pole, 0] + source_ref[lead, :, width:]
        out_ref[pole, 1] = slope_ref[pole, 1] - source_ref[lead, :, :width]


def finish_rows(
    slopes, lead_term, local, received, taken, rho_panel, lead_gamma, pole_lead, first, step
):
    poles, _, _, width = slopes.shape
    rows = local.shape[1]
    smem = pl.BlockSpec(memory_space=SMEM)
    wide = pl.BlockSpec((2, step, 2 * width), lambda i: (0, first // step + i, 0))
    here = pl.BlockSpec((2, step, 2 * width), lambda i: (0, i, 0))
    panel = pl.BlockSpec((poles, 2, step, width), lambda i: (0, 0, first // step + i, 0))
    operands = [pole_lead, taken, lead_gamma, rho_panel, local, received, slopes]
    in_specs = [
        smem,
        smem,
        pl.BlockSpec(lead_gamma.shape, lambda i: (0, 0, 0, 0)),
        wide,
        here,
        here,
        panel,
    ]
    aliases = {6: 0}
    if lead_term is not None:
        operands.append(lead_term)
        in_specs.append(pl.BlockSpec(memory_space=pl.ANY))
        aliases[7] = 1
    return pl.pallas_call(
        finish_kernel,
        grid=(rows // step,),
        in_specs=in_specs,
        out_specs=[panel, wide],
        out_shape=[
            jax.ShapeDtypeStruct(slopes.shape, F32),
            jax.ShapeDtypeStruct(rho_panel.shape, F32),
        ],
        scratch_shapes=[pltpu.VMEM((2, step, 2 * width), F32)],
        input_output_aliases=aliases,
        cost_estimate=pl.CostEstimate(
            flops=12 * rows * (2 * width) ** 2,
            bytes_accessed=16 * poles * rows * width + 64 * rows * width,
            transcendentals=0,
        ),
        name="finish",
    )(*operands)


def fold_chunk(part, axis):
    count = lax.axis_size(axis)
    me = lax.axis_index(axis)
    if count % 2 or count < 4:
        total = lax.psum(part, axis)
        return total, total, jnp.bool_(False)
    inner = count // 2 - 1
    local = part
    for j in range(inner):
        local = local + lax.ppermute(local, axis, [(j, j + 1), (count - 1 - j, count - 2 - j)])
    local = local + lax.ppermute(local, axis, [(inner, inner + 1), (inner + 1, inner)])
    for j in range(inner, 0, -1):
        received = lax.ppermute(local, axis, [(j, j - 1), (count - 1 - j, count - j)])
        taken = (me == j - 1) | (me == count - j)
        if j > 1:
            local = jnp.where(taken, received, local)
    return local, received, taken


def per_device(
    aux_modes,
    rho_panel,
    ham_blocks,
    block_counts,
    block_offsets,
    lead_gamma,
    pole_energy,
    residues,
    pole_lead,
):
    width = ham_blocks.shape[-1]
    rows = aux_modes.shape[2]
    chunk = rows // CHUNKS
    step = 96
    halo = REACH * width

    sums = []
    for c in range(CHUNKS):
        part = mix_rows(aux_modes, pole_lead, residues, c * chunk, chunk, step)
        sums.append(fold_chunk(part, "pole"))

    devices = lax.axis_size("row")
    odd = lax.axis_index("row") % 2
    near_edge = lax.dynamic_slice_in_dim(
        aux_modes, jnp.where(odd == 1, 0, rows - halo), halo, axis=2
    )
    far_edge = lax.dynamic_slice_in_dim(
        aux_modes, jnp.where(odd == 1, rows - halo, 0), halo, axis=2
    )
    near_pairs = [(i, i + 1) for i in range(0, devices - 1, 2)]
    far_pairs = [(i, i + 1) for i in range(1, devices - 1, 2)]
    near = lax.ppermute(near_edge, "row", near_pairs + [(b, a) for a, b in near_pairs])
    far = lax.ppermute(far_edge, "row", far_pairs + [(b, a) for a, b in far_pairs])
    odd = odd.astype(jnp.int32).reshape(1)

    slopes = ham_part(
        aux_modes, near, far, ham_blocks, block_counts, block_offsets, odd, pole_energy
    )
    lead_term = None
    for c, (local, received, taken) in enumerate(sums):
        taken = taken.astype(jnp.int32).reshape(1)
        slopes, lead_term = finish_rows(
            slopes, lead_term, local, received, taken, rho_panel, lead_gamma, pole_lead,
            c * chunk, step,
        )
    return slopes, lead_term


def solution(mesh):
    placed = (
        P(("grp", "pole"), None, "row", None),
        P(None, ("grp", "row"), None),
        P(("grp", "row"), None, None, None, None),
        P(("grp", "row")),
        P(("grp", "row"), None),
        P(),
        P(None, ("grp", "pole")),
        P(None, ("grp", "pole")),
        P(("grp", "pole")),
    )
    return jax.shard_map(
        per_device,
        mesh=mesh,
        in_specs=placed,
        out_specs=(P(("grp", "pole"), None, "row", None), P(None, ("grp", "row"), None)),
        check_vma=False,
    )
```

```python
import functools

import jax
import jax.numpy as jnp
from jax import lax
from jax.experimental import pallas as pl
from jax.experimental.pallas import tpu as pltpu
from jax.sharding import PartitionSpec as P

REACH = 2
FOLDED = 2
F32 = jnp.float32
BF16 = jnp.bfloat16
MIB = 2**20
LIMIT = 10
BIG = 10**10
COSTS = {("add", 1, 0): BIG, ("add", 2, 0): BIG}
WORK_AFTER = (0, 3)
SMEM_SPEC = pl.BlockSpec(memory_space=pltpu.SMEM)
VMEM_SPEC = pl.BlockSpec(memory_space=pltpu.VMEM)
ANY_SPEC = pl.BlockSpec(memory_space=pl.ANY)


def dot(left, right):
    return jnp.dot(left, right, preferred_element_type=F32)


def split_high_low(value):
    high = value.astype(BF16)
    return high, (value - high.astype(F32)).astype(BF16)


def kept(value, place):
    spaces = {"vmem": pltpu.VMEM, "hbm": pltpu.HBM, "smem": pltpu.HBM}
    return pltpu.with_memory_space_constraint(value, spaces[place]) if place in spaces else value


def call(kernel, name, operands, outputs, after=(), scratch=(), aliases=None, through=(), cost=0):
    places = {"smem": SMEM_SPEC, "vmem": VMEM_SPEC, "any": ANY_SPEC, "hbm": ANY_SPEC}
    arrays = [kept(a, place) for a, place in operands]
    passed = [kept(a, place) for a, place in through]
    specs = [places[place] for _, place in operands]
    count = len(operands)
    skipped = len(through) + len(after)
    aliases = dict(aliases or {})
    for i in range(len(through)):
        aliases[count + i] = len(outputs) + i

    def body(*refs):
        refs, outs = refs[:count], refs[count + skipped :]
        kernel(*refs, *outs[: len(outputs)], *outs[len(outputs) + len(through) + 1 :])

    shapes = [
        pltpu.VMEM(shape, dtype) if place == "vmem" else jax.ShapeDtypeStruct(shape, dtype)
        for shape, dtype, place in [*outputs, *((a.shape, a.dtype, place) for a, place in through)]
    ]
    result = pl.pallas_call(
        body,
        in_specs=specs + [places[place] for _, place in through] + [ANY_SPEC] * len(after),
        out_specs=[places[place] for _, _, place in outputs] + [places[place] for _, place in through] + [ANY_SPEC],
        out_shape=shapes + [jax.ShapeDtypeStruct((8, 128), F32)],
        scratch_shapes=list(scratch),
        input_output_aliases=aliases,
        compiler_params=pltpu.CompilerParams(vmem_limit_bytes=LIMIT * MIB),
        cost_estimate=pl.CostEstimate(flops=cost, bytes_accessed=cost, transcendentals=0),
        name=name,
    )(*arrays, *passed, *after)
    return list(result[:-1]), result[-1]


def mix_tile(lead_ref, residue_ref, load, store, poles, width):
    sums = [None] * 4
    for pole in range(poles):
        real, imag = load(pole)
        for lead in range(2):
            alive = (lead_ref[pole] == lead).astype(F32)
            coef_real = alive * residue_ref[0, pole]
            coef_imag = alive * residue_ref[1, pole]
            terms = (
                coef_real * real - coef_imag * imag,
                coef_real * imag + coef_imag * real,
            )
            for part in range(2):
                slot = 2 * part + lead
                sums[slot] = terms[part] if pole == 0 else sums[slot] + terms[part]
    for part in range(2):
        for lead in range(2):
            store(part, slice(lead * width, (lead + 1) * width), sums[2 * part + lead])


def mix_range(lead_ref, residue_ref, aux_ref, out_ref, aux_start, out_start, rows, tile=32):
    poles = aux_ref.shape[0]
    width = aux_ref.shape[-1]
    tile = next(t for t in (tile, 16, 8) if rows % t == 0)

    def step(i, carry):
        at = pl.ds(pl.multiple_of(aux_start + i * tile, 8), tile)
        to = pl.ds(pl.multiple_of(out_start + i * tile, 8), tile)

        def load(pole):
            return aux_ref[pole, 0, at, :], aux_ref[pole, 1, at, :]

        def store(part, columns, value):
            out_ref[part, to, columns] = value

        mix_tile(lead_ref, residue_ref, load, store, poles, width)
        return carry

    lax.fori_loop(0, rows // tile, step, 0)


def first_kernel(rows, lead_ref, residue_ref, aux_ref, out_ref, mode_ref, sems):
    pieces = 2
    size = rows // pieces
    copies = [
        pltpu.make_async_copy(
            aux_ref.at[:, :, pl.ds(i * size, size), :],
            mode_ref.at[:, :, pl.ds(i * size, size), :],
            sems.at[i],
        )
        for i in range(pieces)
    ]
    for copy in copies:
        copy.start()
    for i, copy in enumerate(copies):
        copy.wait()
        mix_range(lead_ref, residue_ref, mode_ref, out_ref, i * size, i * size, size)


def later_kernel(bounds, lead_ref, residue_ref, aux_ref, *rest):
    count = len(bounds) - 1
    outs = rest[: count - 1]
    mode_ref, sems = rest[count - 1 :]
    copies = []
    for c in range(1, count):
        at = pl.ds(bounds[c], bounds[c + 1] - bounds[c])
        to = pl.ds(bounds[c] - bounds[1], bounds[c + 1] - bounds[c])
        copies.append(pltpu.make_async_copy(aux_ref.at[:, :, at, :], mode_ref.at[:, :, to, :], sems.at[c - 1]))
        copies[-1].start()
    for c in range(1, count):
        copies[c - 1].wait()
        mix_range(
            lead_ref, residue_ref, mode_ref, outs[c - 1], bounds[c] - bounds[1], 0, bounds[c + 1] - bounds[c]
        )


def split_kernel(odd_ref, gamma_ref, aux_ref, near_ref, far_ref, high_ref, low_ref, ghigh_ref, glow_ref, mode_ref, sems, edge_sems):
    poles, _, rows, width = aux_ref.shape
    nblock = rows // width
    halo = near_ref.shape[2]
    copies = [
        pltpu.make_async_copy(
            aux_ref.at[:, :, pl.ds(b * width, width), :],
            mode_ref.at[:, :, pl.ds(b * width, width), :],
            sems.at[b],
        )
        for b in range(nblock)
    ]
    outer = [b for b in range(nblock) if b < REACH or b >= nblock - REACH]
    order = outer + [b for b in range(nblock) if b not in outer]
    for b in order:
        copies[b].start()
    for lead in range(2):
        gamma_real = gamma_ref[lead, 0]
        gamma_imag = gamma_ref[lead, 1]
        gamma = jnp.concatenate(
            [
                jnp.concatenate([gamma_real, gamma_imag], axis=1),
                jnp.concatenate([-gamma_imag, gamma_real], axis=1),
            ],
            axis=0,
        )
        ghigh_ref[lead], glow_ref[lead] = split_high_low(gamma)
    odd = odd_ref[0]
    starts = (jnp.where(odd == 1, 0, rows - halo), jnp.where(odd == 1, rows - halo, 0))
    edges = [
        pltpu.make_async_copy(
            mode_ref.at[:, :, pl.ds(pl.multiple_of(start, 128), halo), :], ref, edge_sems.at[i]
        )
        for i, (start, ref) in enumerate(zip(starts, (near_ref, far_ref)))
    ]
    for b in outer:
        copies[b].wait()
    for edge in edges:
        edge.start()
    for b in order:
        if b not in outer:
            copies[b].wait()
        for pole in range(poles):
            for part in range(2):
                high, low = split_high_low(mode_ref[pole, part, pl.ds(b * width, width), :])
                where = (b, pl.ds(part * width, width), pl.ds(pole * width, width))
                high_ref[where] = high
                low_ref[where] = low
    for edge in edges:
        edge.wait()


def add_kernel(left_ref, right_ref, out_ref):
    out_ref[...] = left_ref[...] + right_ref[...]


def pair_split(ham_ref, index, which):
    ham_real = ham_ref[index, which, 0]
    ham_imag = ham_ref[index, which, 1]
    pair = jnp.concatenate(
        [
            jnp.concatenate([ham_real, -ham_imag], axis=1),
            jnp.concatenate([ham_imag, ham_real], axis=1),
        ],
        axis=0,
    )
    return split_high_low(pair)


def product(ham_ref, index, which, high, low):
    pair_high, pair_low = pair_split(ham_ref, index, which)
    return dot(pair_high, high) + dot(pair_high, low) + dot(pair_low, high)


def ham_kernel(first, last, *refs):
    count_ref, offset_ref, energy_ref, ham_ref, aux_ref, high_ref, low_ref = refs[:7]
    out_ref, blocks_ref, mode_ref, total_ref, ham_sems, mode_sems = refs[7:]
    poles, _, rows, width = aux_ref.shape
    nblock = rows // width
    ham_copies = []
    mode_copies = []
    for i, row in enumerate(range(first, last)):
        at = pl.ds(row * width, width)
        ham_copies.append(pltpu.make_async_copy(ham_ref.at[row], blocks_ref.at[i], ham_sems.at[i]))
        mode_copies.append(pltpu.make_async_copy(aux_ref.at[:, :, at, :], mode_ref.at[i], mode_sems.at[i]))
    for copy in ham_copies + mode_copies:
        copy.start()
    for i, row in enumerate(range(first, last)):
        ham_copies[i].wait()
        total_ref[...] = product(blocks_ref, i, 0, high_ref[row], low_ref[row])

        def slot(which, carry):
            place = row + offset_ref[row, which]

            @pl.when((place >= 0) & (place < nblock))
            def _():
                total_ref[...] += product(blocks_ref, i, which, high_ref[place], low_ref[place])

            return carry

        lax.fori_loop(1, count_ref[row], slot, 0)
        mode_copies[i].wait()
        for pole in range(poles):
            real = mode_ref[i, pole, 0]
            imag = mode_ref[i, pole, 1]
            energy_real = energy_ref[0, pole]
            energy_imag = energy_ref[1, pole]
            columns = slice(pole * width, (pole + 1) * width)
            at = pl.ds(i * width, width)
            out_ref[pole, 0, at, :] = total_ref[width:, columns] - (energy_real * imag + energy_imag * real)
            out_ref[pole, 1, at, :] = (energy_real * real - energy_imag * imag) - total_ref[:width, columns]


def ham_part(first, last, aux_modes, high, low, ham_blocks, block_counts, block_offsets, pole_energy, through, after, cost):
    poles, _, rows, width = aux_modes.shape
    slots = ham_blocks.shape[1]
    n = last - first
    operands = [
        (block_counts, "smem"), (block_offsets, "smem"), (pole_energy, "smem"),
        (ham_blocks, "hbm"), (aux_modes, "hbm"), (high, "vmem"), (low, "vmem"),
    ]
    (slopes, *through), token = call(
        functools.partial(ham_kernel, first, last),
        "ham", operands, [((poles, 2, n * width, width), F32, "vmem")], after,
        scratch=[
            pltpu.VMEM((n, slots, 2, width, width), F32),
            pltpu.VMEM((n, poles, 2, width, width), F32),
            pltpu.VMEM((2 * width, poles * width), F32),
            pltpu.SemaphoreType.DMA((n,)),
            pltpu.SemaphoreType.DMA((n,)),
        ],
        through=through,
        cost=cost,
    )
    return slopes, through, token


def edge_kernel(
    nblock, bounds, count_ref, offset_ref, odd_ref, ham_ref, near_ref, far_ref, *refs
):
    pieces = len(bounds)
    ins, outs = refs[:pieces], refs[pieces : 2 * pieces]
    halo_ref, blocks_ref, high_ref, low_ref, total_ref, halo_sems, ham_sems = refs[2 * pieces :]
    poles = near_ref.shape[0]
    width = near_ref.shape[-1]
    odd = odd_ref[0]
    edge_rows = list(range(REACH)) + list(range(nblock - REACH, nblock))
    ham_copies = [
        pltpu.make_async_copy(ham_ref.at[row], blocks_ref.at[i % 2], ham_sems.at[i]) for i, row in enumerate(edge_rows)
    ]
    ham_copies[0].start()
    ham_copies[1].start()
    halo_copies = [
        pltpu.make_async_copy(ref, halo_ref.at[i], halo_sems.at[i]) for i, ref in enumerate((near_ref, far_ref))
    ]
    for copy in halo_copies:
        copy.start()
    for in_ref, out_ref in zip(ins, outs):
        out_ref[...] = in_ref[...]
    for copy in halo_copies:
        copy.wait()
    for i, row in enumerate(edge_rows):
        out_ref, at = next(
            (ref, pl.ds((row - a) * width, width)) for ref, (a, b) in zip(outs, bounds) if a <= row < b
        )
        ham_copies[i].wait()

        def slot(which, carry):
            place = row + offset_ref[row, which]

            @pl.when((place < 0) | (place >= nblock))
            def _():
                below = place < 0
                side = jnp.where(below, 1 - odd, odd)
                start = pl.multiple_of(jnp.where(below, place + REACH, place - nblock) * width, width)
                for pole in range(poles):
                    for part in range(2):
                        high, low = split_high_low(halo_ref[side, pole, part, pl.ds(start, width), :])
                        where = (pl.ds(part * width, width), pl.ds(pole * width, width))
                        high_ref[where] = high
                        low_ref[where] = low
                total_ref[...] = product(blocks_ref, i % 2, which, high_ref[...], low_ref[...])
                for pole in range(poles):
                    columns = slice(pole * width, (pole + 1) * width)
                    out_ref[pole, 0, at, :] += total_ref[width:, columns]
                    out_ref[pole, 1, at, :] -= total_ref[:width, columns]

            return carry

        lax.fori_loop(1, count_ref[row], slot, 0)
        if i + 2 < len(edge_rows):
            ham_copies[i + 2].start()


def edge_part(slopes, bounds, near, far, odd, ham_blocks, block_counts, block_offsets, after):
    nblock, slots = ham_blocks.shape[:2]
    poles, _, _, width = near.shape
    reached = [
        i for i, (a, b) in enumerate(bounds) if a < REACH or b > nblock - REACH
    ]
    outs, token = call(
        functools.partial(edge_kernel, nblock, [bounds[i] for i in reached]), "edge",
        [
            (block_counts, "smem"), (block_offsets, "smem"), (odd, "smem"), (ham_blocks, "hbm"),
            (near, "hbm"), (far, "hbm"),
        ]
        + [(slopes[i], "vmem") for i in reached],
        [(slopes[i].shape, F32, "vmem") for i in reached], after,
        scratch=[
            pltpu.VMEM((2, *near.shape), F32),
            pltpu.VMEM((2, slots, 2, width, width), F32),
            pltpu.VMEM((2 * width, poles * width), BF16),
            pltpu.VMEM((2 * width, poles * width), BF16),
            pltpu.VMEM((2 * width, poles * width), F32),
            pltpu.SemaphoreType.DMA((2,)),
            pltpu.SemaphoreType.DMA((2 * REACH,)),
        ],
    )
    slopes = list(slopes)
    for i, out in zip(reached, outs):
        slopes[i] = out
    return slopes, token


def finish_kernel(first, summed, starts, chained, *refs):
    lead_ref, taken_ref, ghigh_ref, glow_ref, rho_ref, local_ref, received_ref = refs[:7]
    slope_refs = refs[7 : 7 + len(starts)]
    refs = refs[7 + len(starts) + (2 if chained else 0) :]
    out_ref, lead_out_ref, wide_ref, source_ref, panel_ref, sems = refs
    poles, _, _, width = slope_refs[0].shape
    rows = local_ref.shape[1]
    at = pl.ds(first, rows)
    if summed:
        lead_term = local_ref[...] + received_ref[...]
    else:
        lead_term = jnp.where(taken_ref[0] == 1, received_ref[...], local_ref[...])
    wide_ref[...] = lead_term
    copies = [pltpu.make_async_copy(wide_ref, lead_out_ref.at[:, at, :], sems.at[poles])]
    copies[0].start()
    for lead in range(2):
        columns = slice(lead * width, (lead + 1) * width)
        pair = jnp.concatenate(
            [
                rho_ref[part, at, columns] + 0.25 * wide_ref[part, :, columns]
                for part in range(2)
            ],
            axis=1,
        )
        high, low = split_high_low(pair)
        source_ref[lead] = (
            dot(high, ghigh_ref[lead]) + dot(high, glow_ref[lead]) + dot(low, ghigh_ref[lead])
        )
    for pole in range(poles):
        lead = lead_ref[pole]
        for slope_ref, start in zip(slope_refs, starts):
            low_row = max(start, first)
            high_row = min(start + slope_ref.shape[2], first + rows)
            from_ = pl.ds(low_row - start, high_row - low_row)
            to = pl.ds(low_row - first, high_row - low_row)
            panel_ref[pole, 0, to, :] = slope_ref[pole, 0, from_, :] + source_ref[lead, to, width:]
            panel_ref[pole, 1, to, :] = slope_ref[pole, 1, from_, :] - source_ref[lead, to, :width]
        copies.append(
            pltpu.make_async_copy(panel_ref.at[pole], out_ref.at[pole, :, at, :], sems.at[pole])
        )
        copies[-1].start()
    for copy in copies:
        copy.wait()


def finish_rows(
    first, summed, slopes, local, received, taken, rho_panel, ghigh, glow, pole_lead, results, out_shape, after
):
    poles, _, _, width = out_shape
    rows = local.shape[1]
    starts = []
    touched = []
    start = 0
    for piece in slopes:
        if start < first + rows and start + piece.shape[2] > first:
            starts.append(start)
            touched.append((piece, "vmem"))
        start += piece.shape[2]
    operands = [
        (pole_lead, "smem"), (taken, "smem"), (ghigh, "vmem"), (glow, "vmem"), (rho_panel, "vmem"),
        (local, "vmem"), (received, "vmem"), *touched,
    ]
    aliases = None
    if results is not None:
        aliases = {len(operands) + i: i for i in range(2)}
        operands += [(result, "any") for result in results]
    return call(
        functools.partial(finish_kernel, first, summed, starts, results is not None),
        "finish", operands,
        [(out_shape, F32, "any"), (rho_panel.shape, F32, "any")], after,
        scratch=[
            pltpu.VMEM((2, rows, 2 * width), F32),
            pltpu.VMEM((2, rows, 2 * width), F32),
            pltpu.VMEM((poles, 2, rows, width), F32),
            pltpu.SemaphoreType.DMA((poles + 1,)),
        ],
        aliases=aliases,
    )


def per_device(
    aux_modes,
    rho_panel,
    ham_blocks,
    block_counts,
    block_offsets,
    lead_gamma,
    pole_energy,
    residues,
    pole_lead,
):
    poles, _, rows, width = aux_modes.shape
    nblock = rows // width
    halo = REACH * width
    devices = lax.axis_size("row")
    odd = (lax.axis_index("row") % 2).astype(jnp.int32).reshape(1)
    count = lax.axis_size("pole")
    me = lax.axis_index("pole")
    inner = count // 2 - 1
    line = count & (count - 1) == 0 and count >= 4

    swapped = rows // 4
    part_rows = (rows - swapped) // FOLDED
    bounds = [c * part_rows for c in range(FOLDED)] + [rows - swapped, rows]
    chunks = FOLDED + 1
    sizes = [b - a for a, b in zip(bounds, bounds[1:])]

    (part,), token = call(
        functools.partial(first_kernel, sizes[0]), "mix",
        [(pole_lead, "smem"), (residues, "smem"), (aux_modes, "hbm")],
        [((2, sizes[0], 2 * width), F32, "vmem")],
        scratch=[pltpu.VMEM((poles, 2, sizes[0], width), F32), pltpu.SemaphoreType.DMA((2,))],
    )
    later, token = call(
        functools.partial(later_kernel, bounds), "mix_later",
        [(pole_lead, "smem"), (residues, "smem"), (aux_modes, "hbm")],
        [((2, size, 2 * width), F32, "vmem") for size in sizes[1:]],
        [token],
        scratch=[
            pltpu.VMEM((poles, 2, rows - sizes[0], width), F32),
            pltpu.SemaphoreType.DMA((chunks,)),
        ],
    )
    locals_ = [part] + later
    (near_edge, far_edge, high, low, ghigh, glow), token = call(
        split_kernel, "split",
        [(odd, "smem"), (lead_gamma, "vmem"), (aux_modes, "hbm")],
        [((poles, 2, halo, width), F32, "any")] * 2
        + [((nblock, 2 * width, poles * width), BF16, "vmem")] * 2
        + [((2, 2 * width, 2 * width), BF16, "vmem")] * 2,
        [token],
        scratch=[
            pltpu.VMEM(aux_modes.shape, F32),
            pltpu.SemaphoreType.DMA((nblock,)),
            pltpu.SemaphoreType.DMA((2,)),
        ],
    )

    near_pairs = [(i, i + 1) for i in range(0, devices - 1, 2)]
    far_pairs = [(i, i + 1) for i in range(1, devices - 1, 2)]
    received = [None] * chunks
    taken = ((me == 0) | (me == count - 1)).astype(jnp.int32).reshape(1)

    def fold_pairs(stage):
        if stage < inner:
            return [(stage, stage + 1), (count - 1 - stage, count - 2 - stage)]
        if stage == inner:
            return [(inner, inner + 1), (inner + 1, inner)]
        j = 2 * inner + 1 - stage
        return [(j, j - 1), (count - 1 - j, count - j)]

    def send(c, stage):
        if not line:
            received[c] = lax.psum(locals_[c], "pole")
        elif c < FOLDED:
            received[c] = lax.ppermute(locals_[c], "pole", fold_pairs(stage))
        else:
            received[c] = lax.ppermute(locals_[c], "pole", [(i, i ^ (1 << stage)) for i in range(count)])

    def take(c, stage):
        nonlocal token
        if c == FOLDED or stage <= inner:
            (locals_[c],), token = call(
                add_kernel, "add", [(locals_[c], "vmem"), (received[c], "vmem")],
                [(locals_[c].shape, F32, "vmem")], [token], cost=COSTS.get(("add", c, stage), 0),
            )
        else:
            j = 2 * inner + 1 - stage
            target = (me == j - 1) | (me == count - j)
            locals_[c] = jnp.where(target, received[c], locals_[c])

    slopes = []
    results = None
    pieces = [(i * nblock // 3, (i + 1) * nblock // 3) for i in range(3)]
    near = far = None

    def work(piece):
        nonlocal slopes, token, near, far
        through = [(near_edge, "any"), (far_edge, "any")] if piece == 0 else []
        part, through, token = ham_part(
            *pieces[piece], aux_modes, high, low, ham_blocks, block_counts, block_offsets, pole_energy,
            through, [token], COSTS.get(("ham", piece), 0),
        )
        slopes.append(part)
        if piece == 0:
            near = lax.ppermute(through[0], "row", near_pairs + [(b, a) for a, b in near_pairs])
            far = lax.ppermute(through[1], "row", far_pairs + [(b, a) for a, b in far_pairs])

    def reach():
        nonlocal slopes, token
        slopes, token = edge_part(
            slopes, pieces, near, far, odd, ham_blocks, block_counts, block_offsets, [token]
        )

    def finish(c):
        nonlocal results, token
        local = locals_[c] if line else received[c]
        results, token = finish_rows(
            bounds[c], line and c == FOLDED, slopes, local, received[c], taken, rho_panel, ghigh, glow, pole_lead,
            results, aux_modes.shape, [token],
        )

    for c in range(chunks):
        send(c, 0)
    swaps = count.bit_length() - 1
    for step in make_plan(line, inner, swaps, len(pieces)):
        if step[0] == "ham":
            work(step[1])
        elif step[0] == "edge":
            reach()
        elif step[0] == "finish":
            finish(step[1])
        else:
            take(*step)
            send(step[0], step[1] + 1)
    return tuple(results)


def make_plan(line, inner, swaps, pieces):
    if not line:
        return [("ham", i) for i in range(pieces)] + [("edge",)] + [("finish", c) for c in range(FOLDED + 1)]
    plan = []
    for turn in range(FOLDED + 2 * inner - 1):
        plan += [(turn - stage, stage) for stage in range(2 * inner) if 0 <= turn - stage < FOLDED]
    at = plan.index((FOLDED - 1, inner - 1)) + 1
    plan[at:at] = [(FOLDED, stage) for stage in range(swaps - 1)]
    last = plan.pop()
    out = []
    ham = 0
    for i, step in enumerate(plan):
        out.append(step)
        if i in WORK_AFTER:
            out.append(("ham", ham))
            ham += 1
    out += [("ham", i) for i in range(ham, pieces)] + [last, ("edge",)]
    return out + [("finish", c) for c in [*range(FOLDED - 1), FOLDED, FOLDED - 1]]


def solution(mesh):
    placed = (
        P(("grp", "pole"), None, "row", None),
        P(None, ("grp", "row"), None),
        P(("grp", "row"), None, None, None, None),
        P(("grp", "row")),
        P(("grp", "row"), None),
        P(),
        P(None, ("grp", "pole")),
        P(None, ("grp", "pole")),
        P(("grp", "pole")),
    )
    return jax.shard_map(
        per_device,
        mesh=mesh,
        in_specs=placed,
        out_specs=(P(("grp", "pole"), None, "row", None), P(None, ("grp", "row"), None)),
        check_vma=False,
    )
```

```python
import functools

import jax
import jax.numpy as jnp
from jax import lax
from jax.experimental import pallas as pl
from jax.experimental.pallas import tpu as pltpu
from jax.sharding import PartitionSpec as P

REACH = 2
CHUNKS = 3
F32 = jnp.float32
BF16 = jnp.bfloat16
MIB = 2**20
LIMIT = 6
BIG = 10**10
COSTS = {("add", 1, 0): BIG, ("ham", 2): BIG}
SMEM_SPEC = pl.BlockSpec(memory_space=pltpu.SMEM)
VMEM_SPEC = pl.BlockSpec(memory_space=pltpu.VMEM)
ANY_SPEC = pl.BlockSpec(memory_space=pl.ANY)


def dot(left, right):
    return jnp.dot(left, right, preferred_element_type=F32)


def split_high_low(value):
    high = value.astype(BF16)
    return high, (value - high.astype(F32)).astype(BF16)


def kept(value, place):
    spaces = {"vmem": pltpu.VMEM, "hbm": pltpu.HBM, "smem": pltpu.HBM}
    return pltpu.with_memory_space_constraint(value, spaces[place]) if place in spaces else value


def call(kernel, name, operands, outputs, after=(), scratch=(), aliases=None, through=(), cost=0, limit=LIMIT):
    places = {"smem": SMEM_SPEC, "vmem": VMEM_SPEC, "any": ANY_SPEC, "hbm": ANY_SPEC}
    arrays = [kept(a, place) for a, place in operands]
    passed = [kept(a, place) for a, place in through]
    specs = [places[place] for _, place in operands]
    count = len(operands)
    skipped = len(through) + len(after)
    aliases = dict(aliases or {})
    for i in range(len(through)):
        aliases[count + i] = len(outputs) + i

    def body(*refs):
        refs, outs = refs[:count], refs[count + skipped :]
        kernel(*refs, *outs[: len(outputs)], *outs[len(outputs) + len(through) + 1 :])

    shapes = [
        {"vmem": pltpu.VMEM, "hbm": pltpu.HBM}.get(place, jax.ShapeDtypeStruct)(shape, dtype)
        for shape, dtype, place in [*outputs, *((a.shape, a.dtype, place) for a, place in through)]
    ]
    result = pl.pallas_call(
        body,
        in_specs=specs + [places[place] for _, place in through] + [ANY_SPEC] * len(after),
        out_specs=[places[place] for _, _, place in outputs] + [places[place] for _, place in through] + [ANY_SPEC],
        out_shape=shapes + [jax.ShapeDtypeStruct((8, 128), F32)],
        scratch_shapes=list(scratch),
        input_output_aliases=aliases,
        compiler_params=pltpu.CompilerParams(vmem_limit_bytes=limit * MIB),
        cost_estimate=pl.CostEstimate(flops=cost, bytes_accessed=cost, transcendentals=0),
        name=name,
    )(*arrays, *passed, *after)
    return list(result[:-1]), result[-1]


def mix_tile(lead_ref, residue_ref, load, store, poles, width):
    sums = [None] * 4
    for pole in range(poles):
        real, imag = load(pole)
        for lead in range(2):
            alive = (lead_ref[pole] == lead).astype(F32)
            coef_real = alive * residue_ref[0, pole]
            coef_imag = alive * residue_ref[1, pole]
            terms = (
                coef_real * real - coef_imag * imag,
                coef_real * imag + coef_imag * real,
            )
            for part in range(2):
                slot = 2 * part + lead
                sums[slot] = terms[part] if pole == 0 else sums[slot] + terms[part]
    for part in range(2):
        for lead in range(2):
            store(part, slice(lead * width, (lead + 1) * width), sums[2 * part + lead])


def mix_range(lead_ref, residue_ref, aux_ref, out_ref, aux_start, out_start, rows, tile=32):
    poles = aux_ref.shape[0]
    width = aux_ref.shape[-1]
    tile = next(t for t in (tile, 16, 8) if rows % t == 0)

    def step(i, carry):
        at = pl.ds(pl.multiple_of(aux_start + i * tile, 8), tile)
        to = pl.ds(pl.multiple_of(out_start + i * tile, 8), tile)

        def load(pole):
            return aux_ref[pole, 0, at, :], aux_ref[pole, 1, at, :]

        def store(part, columns, value):
            out_ref[part, to, columns] = value

        mix_tile(lead_ref, residue_ref, load, store, poles, width)
        return carry

    lax.fori_loop(0, rows // tile, step, 0)


def first_kernel(first, last, lead_ref, residue_ref, aux_ref, out_ref, mode_ref, sems):
    pieces = 4
    size = (last - first) // pieces
    copies = [
        pltpu.make_async_copy(
            aux_ref.at[:, :, pl.ds(first + i * size, size), :],
            mode_ref.at[:, :, pl.ds(i * size, size), :],
            sems.at[i],
        )
        for i in range(pieces)
    ]
    for copy in copies:
        copy.start()
    for i, copy in enumerate(copies):
        copy.wait()
        mix_range(lead_ref, residue_ref, mode_ref, out_ref, i * size, i * size, size)


def later_kernel(ranges, lead_ref, residue_ref, odd_ref, gamma_ref, aux_ref, *rest):
    outs = rest[: len(ranges)]
    near_ref, far_ref, ghigh_ref, glow_ref, mode_ref, sems, edge_sems = rest[len(ranges) :]
    rows = aux_ref.shape[2]
    halo = near_ref.shape[2]
    copies = []
    place = 0
    places = []
    for i, (first, last) in enumerate(ranges):
        at = pl.ds(first, last - first)
        to = pl.ds(place, last - first)
        copies.append(pltpu.make_async_copy(aux_ref.at[:, :, at, :], mode_ref.at[:, :, to, :], sems.at[i]))
        copies[-1].start()
        places.append(place)
        place += last - first
    for lead in range(2):
        gamma_real = gamma_ref[lead, 0]
        gamma_imag = gamma_ref[lead, 1]
        gamma = jnp.concatenate(
            [
                jnp.concatenate([gamma_real, gamma_imag], axis=1),
                jnp.concatenate([-gamma_imag, gamma_real], axis=1),
            ],
            axis=0,
        )
        ghigh_ref[lead], glow_ref[lead] = split_high_low(gamma)
    odd = odd_ref[0]
    whole = ranges[0] == (0, halo) and ranges[-1] == (rows - halo, rows)
    sides = ((0, 1 - odd), (rows - halo, odd))
    edges = []
    for i, (start, side) in enumerate(sides):
        if whole:
            copies[0 if i == 0 else -1].wait()
            source = mode_ref.at[:, :, pl.ds(places[0 if i == 0 else -1], halo), :]
        else:
            source = aux_ref.at[:, :, pl.ds(start, halo), :]
        for j, ref in enumerate((near_ref, far_ref)):
            edge = pltpu.make_async_copy(source, ref, edge_sems.at[j])
            pl.when(side == j)(edge.start)
        edges.append(pltpu.make_async_copy(source, near_ref, edge_sems.at[i]))
    for i, (first, last) in enumerate(ranges):
        if not (whole and i in (0, len(ranges) - 1)):
            copies[i].wait()
        mix_range(lead_ref, residue_ref, mode_ref, outs[i], places[i], 0, last - first)
    for edge in edges:
        edge.wait()


def add_kernel(left_ref, right_ref, out_ref):
    out_ref[...] = left_ref[...] + right_ref[...]


def pair_split(ham_ref, index, which):
    ham_real = ham_ref[index, which, 0]
    ham_imag = ham_ref[index, which, 1]
    pair = jnp.concatenate(
        [
            jnp.concatenate([ham_real, -ham_imag], axis=1),
            jnp.concatenate([ham_imag, ham_real], axis=1),
        ],
        axis=0,
    )
    return split_high_low(pair)


def product(ham_ref, index, which, mode_ref, place, rows, high_ref, low_ref):
    poles = mode_ref.shape[-4]
    width = mode_ref.shape[-1]
    for pole in range(poles):
        for part in range(2):
            high, low = split_high_low(mode_ref[place, pole, part, rows, :])
            where = (pl.ds(part * width, width), pl.ds(pole * width, width))
            high_ref[where] = high
            low_ref[where] = low
    pair_high, pair_low = pair_split(ham_ref, index, which)
    return dot(pair_high, high_ref[...]) + dot(pair_high, low_ref[...]) + dot(pair_low, high_ref[...])


def ham_kernel(first, last, count_ref, offset_ref, energy_ref, ham_ref, aux_ref, out_ref, blocks_ref, mode_ref, high_ref, low_ref, total_ref, ham_sems, mode_sems):
    poles, _, rows, width = aux_ref.shape
    nblock = rows // width
    slots = ham_ref.shape[1]
    base = max(first - REACH, 0)
    ending = min(last + REACH, nblock)
    own = range(first, last)
    others = [block for block in range(base, ending) if block not in own]
    heads = []
    tails = []
    for i, row in enumerate(own):
        heads.append(pltpu.make_async_copy(ham_ref.at[row, 0], blocks_ref.at[i, 0], ham_sems.at[i, 0]))
        rest = pl.ds(1, slots - 1)
        tails.append(pltpu.make_async_copy(ham_ref.at[row, rest], blocks_ref.at[i, rest], ham_sems.at[i, 1]))
    mode_copies = {
        block: pltpu.make_async_copy(
            aux_ref.at[:, :, pl.ds(block * width, width), :], mode_ref.at[block - base], mode_sems.at[block - base]
        )
        for block in range(base, ending)
    }
    for i, row in enumerate(own):
        heads[i].start()
        mode_copies[row].start()
    for i, row in enumerate(own):
        pl.when(count_ref[row] > 1)(tails[i].start)
    needed = {}
    for block in others:
        uses = [
            (which < count_ref[row]) & (row + offset_ref[row, which] == block)
            for row in own
            for which in range(1, slots)
        ]
        needed[block] = functools.reduce(jnp.logical_or, uses)
        pl.when(needed[block])(mode_copies[block].start)
    whole = pl.ds(0, width)
    for i, row in enumerate(own):
        heads[i].wait()
        mode_copies[row].wait()
        total_ref[i] = product(blocks_ref, i, 0, mode_ref, row - base, whole, high_ref, low_ref)
    for i, row in enumerate(own):
        pl.when(count_ref[row] > 1)(tails[i].wait)
    for block in others:
        pl.when(needed[block])(mode_copies[block].wait)
    for i, row in enumerate(own):

        def slot(which, carry):
            place = row + offset_ref[row, which]

            @pl.when((place >= 0) & (place < nblock))
            def _():
                total_ref[i] += product(blocks_ref, i, which, mode_ref, place - base, whole, high_ref, low_ref)

            return carry

        lax.fori_loop(1, count_ref[row], slot, 0)
        for pole in range(poles):
            real = mode_ref[row - base, pole, 0]
            imag = mode_ref[row - base, pole, 1]
            energy_real = energy_ref[0, pole]
            energy_imag = energy_ref[1, pole]
            columns = slice(pole * width, (pole + 1) * width)
            at = pl.ds(i * width, width)
            out_ref[pole, 0, at, :] = total_ref[i, width:, columns] - (energy_real * imag + energy_imag * real)
            out_ref[pole, 1, at, :] = (energy_real * real - energy_imag * imag) - total_ref[i, :width, columns]


def ham_part(first, last, aux_modes, ham_blocks, block_counts, block_offsets, pole_energy, after, cost):
    poles, _, rows, width = aux_modes.shape
    nblock, slots = ham_blocks.shape[:2]
    n = last - first
    held = min(last + REACH, nblock) - max(first - REACH, 0)
    (slopes,), token = call(
        functools.partial(ham_kernel, first, last),
        "ham",
        [
            (block_counts, "smem"), (block_offsets, "smem"), (pole_energy, "smem"),
            (ham_blocks, "hbm"), (aux_modes, "hbm"),
        ],
        [((poles, 2, n * width, width), F32, "vmem")], after,
        scratch=[
            pltpu.VMEM((n, slots, 2, width, width), F32),
            pltpu.VMEM((held, poles, 2, width, width), F32),
            pltpu.VMEM((2 * width, poles * width), BF16),
            pltpu.VMEM((2 * width, poles * width), BF16),
            pltpu.VMEM((n, 2 * width, poles * width), F32),
            pltpu.SemaphoreType.DMA((n, 2)),
            pltpu.SemaphoreType.DMA((held,)),
        ],
        cost=cost,
        limit=14,
    )
    return slopes, token


def edge_kernel(nblock, bounds, count_ref, offset_ref, odd_ref, ham_ref, near_ref, far_ref, *refs):
    pieces = len(bounds)
    ins, outs = refs[:pieces], refs[pieces : 2 * pieces]
    blocks_ref, high_ref, low_ref, total_ref, ham_sems = refs[2 * pieces :]
    poles = near_ref.shape[1]
    width = near_ref.shape[-1]
    odd = odd_ref[0]
    edge_rows = list(range(REACH)) + list(range(nblock - REACH, nblock))
    ham_copies = [
        pltpu.make_async_copy(ham_ref.at[row], blocks_ref.at[i], ham_sems.at[i]) for i, row in enumerate(edge_rows)
    ]
    for copy in ham_copies:
        copy.start()
    for in_ref, out_ref in zip(ins, outs):
        out_ref[...] = in_ref[...]
    for i, row in enumerate(edge_rows):
        out_ref, at = next(
            (ref, pl.ds((row - a) * width, width)) for ref, (a, b) in zip(outs, bounds) if a <= row < b
        )
        ham_copies[i].wait()

        def slot(which, carry):
            place = row + offset_ref[row, which]
            below = place < 0
            above = place >= nblock
            start = pl.multiple_of(jnp.where(below, place + REACH, place - nblock) * width, width)

            def add(halo_ref):
                total_ref[...] = product(blocks_ref, i, which, halo_ref, 0, pl.ds(start, width), high_ref, low_ref)
                for pole in range(poles):
                    columns = slice(pole * width, (pole + 1) * width)
                    out_ref[pole, 0, at, :] += total_ref[width:, columns]
                    out_ref[pole, 1, at, :] -= total_ref[:width, columns]

            pl.when((below & (odd == 1)) | (above & (odd == 0)))(lambda: add(near_ref))
            pl.when((below & (odd == 0)) | (above & (odd == 1)))(lambda: add(far_ref))
            return carry

        lax.fori_loop(1, count_ref[row], slot, 0)


def edge_part(slopes, bounds, near, far, odd, ham_blocks, block_counts, block_offsets, after):
    nblock, slots = ham_blocks.shape[:2]
    poles, _, _, width = near.shape
    reached = [i for i, (a, b) in enumerate(bounds) if a < REACH or b > nblock - REACH]
    outs, token = call(
        functools.partial(edge_kernel, nblock, [bounds[i] for i in reached]), "edge",
        [
            (block_counts, "smem"), (block_offsets, "smem"), (odd, "smem"), (ham_blocks, "hbm"),
            (near[None], "vmem"), (far[None], "vmem"),
        ]
        + [(slopes[i], "vmem") for i in reached],
        [(slopes[i].shape, F32, "vmem") for i in reached], after,
        scratch=[
            pltpu.VMEM((2 * REACH, slots, 2, width, width), F32),
            pltpu.VMEM((2 * width, poles * width), BF16),
            pltpu.VMEM((2 * width, poles * width), BF16),
            pltpu.VMEM((2 * width, poles * width), F32),
            pltpu.SemaphoreType.DMA((2 * REACH,)),
        ],
        limit=8,
    )
    slopes = list(slopes)
    for i, out in zip(reached, outs):
        slopes[i] = out
    return slopes, token


def finish_kernel(first, starts, chained, *refs):
    lead_ref, taken_ref, ghigh_ref, glow_ref, rho_ref, local_ref, received_ref = refs[:7]
    slope_refs = refs[7 : 7 + len(starts)]
    refs = refs[7 + len(starts) + (2 if chained else 0) :]
    out_ref, lead_out_ref, wide_ref, source_ref, panel_ref, sems = refs
    poles, _, _, width = slope_refs[0].shape
    rows = local_ref.shape[1]
    at = pl.ds(first, rows)
    lead_term = jnp.where(taken_ref[0] == 1, received_ref[...], local_ref[...])
    wide_ref[...] = lead_term
    copies = [pltpu.make_async_copy(wide_ref, lead_out_ref.at[:, at, :], sems.at[poles])]
    copies[0].start()
    for lead in range(2):
        columns = slice(lead * width, (lead + 1) * width)
        pair = jnp.concatenate(
            [
                rho_ref[part, at, columns] + 0.25 * wide_ref[part, :, columns]
                for part in range(2)
            ],
            axis=1,
        )
        high, low = split_high_low(pair)
        source_ref[lead] = (
            dot(high, ghigh_ref[lead]) + dot(high, glow_ref[lead]) + dot(low, ghigh_ref[lead])
        )
    for pole in range(poles):
        lead = lead_ref[pole]
        for slope_ref, start in zip(slope_refs, starts):
            low_row = max(start, first)
            high_row = min(start + slope_ref.shape[2], first + rows)
            from_ = pl.ds(low_row - start, high_row - low_row)
            to = pl.ds(low_row - first, high_row - low_row)
            panel_ref[pole, 0, to, :] = slope_ref[pole, 0, from_, :] + source_ref[lead, to, width:]
            panel_ref[pole, 1, to, :] = slope_ref[pole, 1, from_, :] - source_ref[lead, to, :width]
        copies.append(
            pltpu.make_async_copy(panel_ref.at[pole], out_ref.at[pole, :, at, :], sems.at[pole])
        )
        copies[-1].start()
    for copy in copies:
        copy.wait()


def finish_rows(
    first, slopes, pieces, local, received, taken, rho_panel, ghigh, glow, pole_lead, results, out_shape, after, cost
):
    poles, _, _, width = out_shape
    rows = local.shape[1]
    starts = []
    touched = []
    for piece, (a, b) in zip(slopes, pieces):
        if a * width < first + rows and b * width > first:
            starts.append(a * width)
            touched.append((piece, "vmem"))
    operands = [
        (pole_lead, "smem"), (taken, "smem"), (ghigh, "vmem"), (glow, "vmem"), (rho_panel, "vmem"),
        (local, "vmem"), (received, "vmem"), *touched,
    ]
    aliases = None
    if results is not None:
        aliases = {len(operands) + i: i for i in range(2)}
        operands += [(result, "any") for result in results]
    return call(
        functools.partial(finish_kernel, first, starts, results is not None),
        "finish", operands,
        [(out_shape, F32, "any"), (rho_panel.shape, F32, "any")], after,
        scratch=[
            pltpu.VMEM((2, rows, 2 * width), F32),
            pltpu.VMEM((2, rows, 2 * width), F32),
            pltpu.VMEM((poles, 2, rows, width), F32),
            pltpu.SemaphoreType.DMA((poles + 1,)),
        ],
        aliases=aliases,
        cost=cost,
    )


def per_device(
    aux_modes,
    rho_panel,
    ham_blocks,
    block_counts,
    block_offsets,
    lead_gamma,
    pole_energy,
    residues,
    pole_lead,
):
    poles, _, rows, width = aux_modes.shape
    nblock = rows // width
    halo = REACH * width
    devices = lax.axis_size("row")
    odd = (lax.axis_index("row") % 2).astype(jnp.int32).reshape(1)
    count = lax.axis_size("pole")
    me = lax.axis_index("pole")
    inner = count // 2 - 1
    line = count % 2 == 0 and count >= 4

    chunks = CHUNKS
    ranges = [(c * rows // chunks, (c + 1) * rows // chunks) for c in range(chunks)]
    ranges = [ranges[1], ranges[0], *ranges[2:]]
    sizes = [b - a for a, b in ranges]

    (part,), token = call(
        functools.partial(first_kernel, *ranges[0]), "mix",
        [(pole_lead, "smem"), (residues, "smem"), (aux_modes, "hbm")],
        [((2, sizes[0], 2 * width), F32, "vmem")],
        scratch=[pltpu.VMEM((poles, 2, sizes[0], width), F32), pltpu.SemaphoreType.DMA((4,))],
    )
    later, token = call(
        functools.partial(later_kernel, ranges[1:]), "mix_later",
        [(pole_lead, "smem"), (residues, "smem"), (odd, "smem"), (lead_gamma, "vmem"), (aux_modes, "hbm")],
        [((2, size, 2 * width), F32, "vmem") for size in sizes[1:]]
        + [((poles, 2, halo, width), F32, "hbm")] * 2
        + [((2, 2 * width, 2 * width), BF16, "vmem")] * 2,
        [token],
        scratch=[
            pltpu.VMEM((poles, 2, rows - sizes[0], width), F32),
            pltpu.SemaphoreType.DMA((chunks,)),
            pltpu.SemaphoreType.DMA((2,)),
        ],
    )
    near_edge, far_edge, ghigh, glow = later[chunks - 1 :]
    locals_ = [part] + later[: chunks - 1]

    near_pairs = [(i, i + 1) for i in range(0, devices - 1, 2)]
    far_pairs = [(i, i + 1) for i in range(1, devices - 1, 2)]
    received = [None] * chunks
    taken = ((me == 0) | (me == count - 1)).astype(jnp.int32).reshape(1)

    def fold_pairs(stage):
        if stage < inner:
            return [(stage, stage + 1), (count - 1 - stage, count - 2 - stage)]
        if stage == inner:
            return [(inner, inner + 1), (inner + 1, inner)]
        j = 2 * inner + 1 - stage
        return [(j, j - 1), (count - 1 - j, count - j)]

    def send(c, stage):
        if line:
            received[c] = lax.ppermute(locals_[c], "pole", fold_pairs(stage))
        else:
            received[c] = lax.psum(locals_[c], "pole")

    def take(c, stage):
        nonlocal token
        if stage <= inner:
            (locals_[c],), token = call(
                add_kernel, "add", [(locals_[c], "vmem"), (received[c], "vmem")],
                [(locals_[c].shape, F32, "vmem")], [token], cost=COSTS.get(("add", c, stage), 0),
            )
        else:
            j = 2 * inner + 1 - stage
            target = (me == j - 1) | (me == count - j)
            locals_[c] = jnp.where(target, received[c], locals_[c])

    slopes = [None] * 3
    results = None
    pieces = [(i * nblock // 3, (i + 1) * nblock // 3) for i in range(3)]
    near = far = None

    def work(piece):
        nonlocal token
        slopes[piece], token = ham_part(
            *pieces[piece], aux_modes, ham_blocks, block_counts, block_offsets, pole_energy,
            [token], COSTS.get(("ham", piece), 0),
        )

    def neighbours():
        nonlocal near, far, token
        (near, far), token = call(
            lambda: None, "pass", [], [], [token], through=[(near_edge, "hbm"), (far_edge, "hbm")]
        )
        near = lax.ppermute(near, "row", near_pairs + [(b, a) for a, b in near_pairs])
        far = lax.ppermute(far, "row", far_pairs + [(b, a) for a, b in far_pairs])

    def reach():
        nonlocal slopes, token
        slopes, token = edge_part(
            slopes, pieces, near, far, odd, ham_blocks, block_counts, block_offsets, [token]
        )

    def finish(c):
        nonlocal results, token
        local = locals_[c] if line else received[c]
        results, token = finish_rows(
            ranges[c][0], slopes, pieces, local, received[c], taken, rho_panel, ghigh, glow, pole_lead,
            results, aux_modes.shape, [token], COSTS.get(("finish", c), 0),
        )

    for c in range(chunks):
        send(c, 0)
    for step in make_plan(line, 2 * inner, len(pieces)):
        if step[0] == "ham":
            work(step[1])
        elif step[0] == "edge":
            reach()
        elif step[0] == "pass":
            neighbours()
        elif step[0] == "finish":
            finish(step[1])
        else:
            take(*step)
            send(step[0], step[1] + 1)
    return tuple(results)


def make_plan(line, stages, pieces):
    work = [("ham", i) for i in [1, 0, *range(2, pieces)]]
    ending = [("edge",)] + [("finish", c) for c in range(1, CHUNKS)]
    plan = [work.pop(0)]
    if not line:
        return plan + [("pass",)] + work + [("finish", 0)] + ending
    for turn in range(CHUNKS + stages - 1):
        for stage in range(stages):
            if 0 <= turn - stage < CHUNKS:
                plan.append((turn - stage, stage))
            if turn == stage == 0:
                plan.append(("pass",))
        if turn == CHUNKS - 1:
            plan.append(("finish", 0))
        if turn > 0 and work:
            plan.append(work.pop(0))
    return plan + work + ending


def solution(mesh):
    placed = (
        P(("grp", "pole"), None, "row", None),
        P(None, ("grp", "row"), None),
        P(("grp", "row"), None, None, None, None),
        P(("grp", "row")),
        P(("grp", "row"), None),
        P(),
        P(None, ("grp", "pole")),
        P(None, ("grp", "pole")),
        P(("grp", "pole")),
    )
    return jax.shard_map(
        per_device,
        mesh=mesh,
        in_specs=placed,
        out_specs=(P(("grp", "pole"), None, "row", None), P(None, ("grp", "row"), None)),
        check_vma=False,
    )
```

```python
import functools

import jax
import jax.numpy as jnp
from jax import lax
from jax.experimental import pallas as pl
from jax.experimental.pallas import tpu as pltpu
from jax.sharding import PartitionSpec as P

REACH = 2
CHUNKS = 3
F32 = jnp.float32
BF16 = jnp.bfloat16
MIB = 2**20
LIMIT = 6
BIG = 10**10
COSTS = {("add", 1, 0): BIG, ("finish", 0): BIG}
SMEM_SPEC = pl.BlockSpec(memory_space=pltpu.SMEM)
VMEM_SPEC = pl.BlockSpec(memory_space=pltpu.VMEM)
ANY_SPEC = pl.BlockSpec(memory_space=pl.ANY)


def dot(left, right):
    return jnp.dot(left, right, preferred_element_type=F32)


def split_high_low(value):
    high = value.astype(BF16)
    return high, (value - high.astype(F32)).astype(BF16)


def kept(value, place):
    spaces = {"vmem": pltpu.VMEM, "hbm": pltpu.HBM, "smem": pltpu.HBM}
    return pltpu.with_memory_space_constraint(value, spaces[place]) if place in spaces else value


def call(kernel, name, operands, outputs, after=(), scratch=(), aliases=None, through=(), cost=0, limit=LIMIT):
    places = {"smem": SMEM_SPEC, "vmem": VMEM_SPEC, "any": ANY_SPEC, "hbm": ANY_SPEC}
    arrays = [kept(a, place) for a, place in operands]
    passed = [kept(a, place) for a, place in through]
    specs = [places[place] for _, place in operands]
    count = len(operands)
    skipped = len(through) + len(after)
    aliases = dict(aliases or {})
    for i in range(len(through)):
        aliases[count + i] = len(outputs) + i

    def body(*refs):
        refs, outs = refs[:count], refs[count + skipped :]
        kernel(*refs, *outs[: len(outputs)], *outs[len(outputs) + len(through) + 1 :])

    shapes = [
        {"vmem": pltpu.VMEM, "hbm": pltpu.HBM}.get(place, jax.ShapeDtypeStruct)(shape, dtype)
        for shape, dtype, place in [*outputs, *((a.shape, a.dtype, place) for a, place in through)]
    ]
    result = pl.pallas_call(
        body,
        in_specs=specs + [places[place] for _, place in through] + [ANY_SPEC] * len(after),
        out_specs=[places[place] for _, _, place in outputs] + [places[place] for _, place in through] + [ANY_SPEC],
        out_shape=shapes + [jax.ShapeDtypeStruct((8, 128), F32)],
        scratch_shapes=list(scratch),
        input_output_aliases=aliases,
        compiler_params=pltpu.CompilerParams(vmem_limit_bytes=limit * MIB),
        cost_estimate=pl.CostEstimate(flops=cost, bytes_accessed=cost, transcendentals=0),
        name=name,
    )(*arrays, *passed, *after)
    return list(result[:-1]), result[-1]


def mix_tile(lead_ref, residue_ref, load, store, poles, width):
    sums = [None] * 4
    for pole in range(poles):
        real, imag = load(pole)
        for lead in range(2):
            alive = (lead_ref[pole] == lead).astype(F32)
            coef_real = alive * residue_ref[0, pole]
            coef_imag = alive * residue_ref[1, pole]
            terms = (
                coef_real * real - coef_imag * imag,
                coef_real * imag + coef_imag * real,
            )
            for part in range(2):
                slot = 2 * part + lead
                sums[slot] = terms[part] if pole == 0 else sums[slot] + terms[part]
    for part in range(2):
        for lead in range(2):
            store(part, slice(lead * width, (lead + 1) * width), sums[2 * part + lead])


def mix_range(lead_ref, residue_ref, aux_ref, out_ref, aux_start, out_start, rows, tile=32):
    poles = aux_ref.shape[0]
    width = aux_ref.shape[-1]
    tile = next(t for t in (tile, 16, 8) if rows % t == 0)

    def step(i, carry):
        at = pl.ds(pl.multiple_of(aux_start + i * tile, 8), tile)
        to = pl.ds(pl.multiple_of(out_start + i * tile, 8), tile)

        def load(pole):
            return aux_ref[pole, 0, at, :], aux_ref[pole, 1, at, :]

        def store(part, columns, value):
            out_ref[part, to, columns] = value

        mix_tile(lead_ref, residue_ref, load, store, poles, width)
        return carry

    lax.fori_loop(0, rows // tile, step, 0)


def first_kernel(first, last, sends_ref, lead_ref, residue_ref, aux_ref, out_ref, mode_ref, sems):
    pieces = 4
    size = (last - first) // pieces
    copies = [
        pltpu.make_async_copy(
            aux_ref.at[:, :, pl.ds(first + i * size, size), :],
            mode_ref.at[:, :, pl.ds(i * size, size), :],
            sems.at[i],
        )
        for i in range(pieces)
    ]

    @pl.when(sends_ref[0] == 1)
    def _():
        for copy in copies:
            copy.start()
        for i, copy in enumerate(copies):
            copy.wait()
            mix_range(lead_ref, residue_ref, mode_ref, out_ref, i * size, i * size, size)


def later_kernel(ranges, lead_ref, residue_ref, odd_ref, gamma_ref, aux_ref, *rest):
    outs = rest[: len(ranges)]
    near_ref, far_ref, ghigh_ref, glow_ref, mode_ref, sems, edge_sems = rest[len(ranges) :]
    rows = aux_ref.shape[2]
    halo = near_ref.shape[2]
    copies = []
    place = 0
    places = []
    for i, (first, last) in enumerate(ranges):
        at = pl.ds(first, last - first)
        to = pl.ds(place, last - first)
        copies.append(pltpu.make_async_copy(aux_ref.at[:, :, at, :], mode_ref.at[:, :, to, :], sems.at[i]))
        places.append(place)
        place += last - first
    order = [*range(1, len(ranges)), 0]
    for i in order:
        copies[i].start()
    for lead in range(2):
        gamma_real = gamma_ref[lead, 0]
        gamma_imag = gamma_ref[lead, 1]
        gamma = jnp.concatenate(
            [
                jnp.concatenate([gamma_real, gamma_imag], axis=1),
                jnp.concatenate([-gamma_imag, gamma_real], axis=1),
            ],
            axis=0,
        )
        ghigh_ref[lead], glow_ref[lead] = split_high_low(gamma)
    odd = odd_ref[0]
    held = [(0, halo), (rows - halo, rows)]
    whole = all(side in ranges for side in held)
    sides = ((0, 1 - odd), (rows - halo, odd))
    edges = []
    for i, (start, side) in enumerate(sides):
        if whole:
            copies[ranges.index(held[i])].wait()
            source = mode_ref.at[:, :, pl.ds(places[ranges.index(held[i])], halo), :]
        else:
            source = aux_ref.at[:, :, pl.ds(start, halo), :]
        for j, ref in enumerate((near_ref, far_ref)):
            edge = pltpu.make_async_copy(source, ref, edge_sems.at[j])
            pl.when(side == j)(edge.start)
        edges.append(pltpu.make_async_copy(source, near_ref, edge_sems.at[i]))
    for i in order:
        first, last = ranges[i]
        if not (whole and ranges[i] in held):
            copies[i].wait()
        mix_range(lead_ref, residue_ref, mode_ref, outs[i], places[i], 0, last - first)
    for edge in edges:
        edge.wait()


def add_kernel(left_ref, right_ref, out_ref):
    out_ref[...] = left_ref[...] + right_ref[...]


def pair_split(ham_ref, index, which):
    ham_real = ham_ref[index, which, 0]
    ham_imag = ham_ref[index, which, 1]
    pair = jnp.concatenate(
        [
            jnp.concatenate([ham_real, -ham_imag], axis=1),
            jnp.concatenate([ham_imag, ham_real], axis=1),
        ],
        axis=0,
    )
    return split_high_low(pair)


def product(ham_ref, index, which, mode_ref, place, rows, high_ref, low_ref):
    poles = mode_ref.shape[-4]
    width = mode_ref.shape[-1]
    for pole in range(poles):
        for part in range(2):
            high, low = split_high_low(mode_ref[place, pole, part, rows, :])
            where = (pl.ds(part * width, width), pl.ds(pole * width, width))
            high_ref[where] = high
            low_ref[where] = low
    pair_high, pair_low = pair_split(ham_ref, index, which)
    return dot(pair_high, high_ref[...]) + dot(pair_high, low_ref[...]) + dot(pair_low, high_ref[...])


def ham_kernel(first, last, count_ref, offset_ref, energy_ref, ham_ref, aux_ref, out_ref, blocks_ref, mode_ref, high_ref, low_ref, total_ref, ham_sems, mode_sems):
    poles, _, rows, width = aux_ref.shape
    nblock = rows // width
    slots = ham_ref.shape[1]
    base = max(first - REACH, 0)
    ending = min(last + REACH, nblock)
    own = range(first, last)
    others = [block for block in range(base, ending) if block not in own]
    heads = []
    tails = []
    for i, row in enumerate(own):
        heads.append(pltpu.make_async_copy(ham_ref.at[row, 0], blocks_ref.at[i, 0], ham_sems.at[i, 0]))
        rest = pl.ds(1, slots - 1)
        tails.append(pltpu.make_async_copy(ham_ref.at[row, rest], blocks_ref.at[i, rest], ham_sems.at[i, 1]))
    mode_copies = {
        block: pltpu.make_async_copy(
            aux_ref.at[:, :, pl.ds(block * width, width), :], mode_ref.at[block - base], mode_sems.at[block - base]
        )
        for block in range(base, ending)
    }
    for i, row in enumerate(own):
        heads[i].start()
        mode_copies[row].start()
    for i, row in enumerate(own):
        pl.when(count_ref[row] > 1)(tails[i].start)
    needed = {}
    for block in others:
        uses = [
            (which < count_ref[row]) & (row + offset_ref[row, which] == block)
            for row in own
            for which in range(1, slots)
        ]
        needed[block] = functools.reduce(jnp.logical_or, uses)
        pl.when(needed[block])(mode_copies[block].start)
    whole = pl.ds(0, width)
    for i, row in enumerate(own):
        heads[i].wait()
        mode_copies[row].wait()
        total_ref[i] = product(blocks_ref, i, 0, mode_ref, row - base, whole, high_ref, low_ref)
    for i, row in enumerate(own):
        pl.when(count_ref[row] > 1)(tails[i].wait)
    for block in others:
        pl.when(needed[block])(mode_copies[block].wait)
    for i, row in enumerate(own):

        def slot(which, carry):
            place = row + offset_ref[row, which]

            @pl.when((place >= 0) & (place < nblock))
            def _():
                total_ref[i] += product(blocks_ref, i, which, mode_ref, place - base, whole, high_ref, low_ref)

            return carry

        lax.fori_loop(1, count_ref[row], slot, 0)
        for pole in range(poles):
            real = mode_ref[row - base, pole, 0]
            imag = mode_ref[row - base, pole, 1]
            energy_real = energy_ref[0, pole]
            energy_imag = energy_ref[1, pole]
            columns = slice(pole * width, (pole + 1) * width)
            at = pl.ds(i * width, width)
            out_ref[pole, 0, at, :] = total_ref[i, width:, columns] - (energy_real * imag + energy_imag * real)
            out_ref[pole, 1, at, :] = (energy_real * real - energy_imag * imag) - total_ref[i, :width, columns]


def ham_part(first, last, aux_modes, ham_blocks, block_counts, block_offsets, pole_energy, after, cost):
    poles, _, rows, width = aux_modes.shape
    nblock, slots = ham_blocks.shape[:2]
    n = last - first
    held = min(last + REACH, nblock) - max(first - REACH, 0)
    (slopes,), token = call(
        functools.partial(ham_kernel, first, last),
        "ham",
        [
            (block_counts, "smem"), (block_offsets, "smem"), (pole_energy, "smem"),
            (ham_blocks, "hbm"), (aux_modes, "hbm"),
        ],
        [((poles, 2, n * width, width), F32, "vmem")], after,
        scratch=[
            pltpu.VMEM((n, slots, 2, width, width), F32),
            pltpu.VMEM((held, poles, 2, width, width), F32),
            pltpu.VMEM((2 * width, poles * width), BF16),
            pltpu.VMEM((2 * width, poles * width), BF16),
            pltpu.VMEM((n, 2 * width, poles * width), F32),
            pltpu.SemaphoreType.DMA((n, 2)),
            pltpu.SemaphoreType.DMA((held,)),
        ],
        cost=cost,
        limit=14,
    )
    return slopes, token


def edge_kernel(nblock, bounds, count_ref, offset_ref, odd_ref, ham_ref, near_ref, far_ref, *refs):
    pieces = len(bounds)
    ins, outs = refs[:pieces], refs[pieces : 2 * pieces]
    blocks_ref, high_ref, low_ref, total_ref, ham_sems = refs[2 * pieces :]
    poles = near_ref.shape[1]
    width = near_ref.shape[-1]
    odd = odd_ref[0]
    edge_rows = list(range(REACH)) + list(range(nblock - REACH, nblock))
    ham_copies = [
        pltpu.make_async_copy(ham_ref.at[row], blocks_ref.at[i], ham_sems.at[i]) for i, row in enumerate(edge_rows)
    ]
    for copy in ham_copies:
        copy.start()
    for in_ref, out_ref in zip(ins, outs):
        out_ref[...] = in_ref[...]
    for i, row in enumerate(edge_rows):
        out_ref, at = next(
            (ref, pl.ds((row - a) * width, width)) for ref, (a, b) in zip(outs, bounds) if a <= row < b
        )
        ham_copies[i].wait()

        def slot(which, carry):
            place = row + offset_ref[row, which]
            below = place < 0
            above = place >= nblock
            start = pl.multiple_of(jnp.where(below, place + REACH, place - nblock) * width, width)

            def add(halo_ref):
                total_ref[...] = product(blocks_ref, i, which, halo_ref, 0, pl.ds(start, width), high_ref, low_ref)
                for pole in range(poles):
                    columns = slice(pole * width, (pole + 1) * width)
                    out_ref[pole, 0, at, :] += total_ref[width:, columns]
                    out_ref[pole, 1, at, :] -= total_ref[:width, columns]

            pl.when((below & (odd == 1)) | (above & (odd == 0)))(lambda: add(near_ref))
            pl.when((below & (odd == 0)) | (above & (odd == 1)))(lambda: add(far_ref))
            return carry

        lax.fori_loop(1, count_ref[row], slot, 0)


def edge_part(slopes, bounds, near, far, odd, ham_blocks, block_counts, block_offsets, after):
    nblock, slots = ham_blocks.shape[:2]
    poles, _, _, width = near.shape
    reached = [i for i, (a, b) in enumerate(bounds) if a < REACH or b > nblock - REACH]
    outs, token = call(
        functools.partial(edge_kernel, nblock, [bounds[i] for i in reached]), "edge",
        [
            (block_counts, "smem"), (block_offsets, "smem"), (odd, "smem"), (ham_blocks, "hbm"),
            (near[None], "vmem"), (far[None], "vmem"),
        ]
        + [(slopes[i], "vmem") for i in reached],
        [(slopes[i].shape, F32, "vmem") for i in reached], after,
        scratch=[
            pltpu.VMEM((2 * REACH, slots, 2, width, width), F32),
            pltpu.VMEM((2 * width, poles * width), BF16),
            pltpu.VMEM((2 * width, poles * width), BF16),
            pltpu.VMEM((2 * width, poles * width), F32),
            pltpu.SemaphoreType.DMA((2 * REACH,)),
        ],
        limit=8,
    )
    slopes = list(slopes)
    for i, out in zip(reached, outs):
        slopes[i] = out
    return slopes, token


def finish_kernel(first, starts, chained, *refs):
    lead_ref, taken_ref, ghigh_ref, glow_ref, rho_ref, local_ref, received_ref = refs[:7]
    slope_refs = refs[7 : 7 + len(starts)]
    refs = refs[7 + len(starts) + (2 if chained else 0) :]
    out_ref, lead_out_ref, wide_ref, source_ref, panel_ref, sems = refs
    poles, _, _, width = slope_refs[0].shape
    rows = local_ref.shape[1]
    at = pl.ds(first, rows)
    lead_term = jnp.where(taken_ref[0] == 1, received_ref[...], local_ref[...])
    wide_ref[...] = lead_term
    copies = [pltpu.make_async_copy(wide_ref, lead_out_ref.at[:, at, :], sems.at[poles])]
    copies[0].start()
    for lead in range(2):
        columns = slice(lead * width, (lead + 1) * width)
        pair = jnp.concatenate(
            [
                rho_ref[part, at, columns] + 0.25 * wide_ref[part, :, columns]
                for part in range(2)
            ],
            axis=1,
        )
        high, low = split_high_low(pair)
        source_ref[lead] = (
            dot(high, ghigh_ref[lead]) + dot(high, glow_ref[lead]) + dot(low, ghigh_ref[lead])
        )
    for pole in range(poles):
        lead = lead_ref[pole]
        for slope_ref, start in zip(slope_refs, starts):
            low_row = max(start, first)
            high_row = min(start + slope_ref.shape[2], first + rows)
            from_ = pl.ds(low_row - start, high_row - low_row)
            to = pl.ds(low_row - first, high_row - low_row)
            panel_ref[pole, 0, to, :] = slope_ref[pole, 0, from_, :] + source_ref[lead, to, width:]
            panel_ref[pole, 1, to, :] = slope_ref[pole, 1, from_, :] - source_ref[lead, to, :width]
        copies.append(
            pltpu.make_async_copy(panel_ref.at[pole], out_ref.at[pole, :, at, :], sems.at[pole])
        )
        copies[-1].start()
    for copy in copies:
        copy.wait()


def finish_rows(
    first, slopes, pieces, local, received, taken, rho_panel, ghigh, glow, pole_lead, results, out_shape, after, cost
):
    poles, _, _, width = out_shape
    rows = local.shape[1]
    starts = []
    touched = []
    for piece, (a, b) in zip(slopes, pieces):
        if a * width < first + rows and b * width > first:
            starts.append(a * width)
            touched.append((piece, "vmem"))
    operands = [
        (pole_lead, "smem"), (taken, "smem"), (ghigh, "vmem"), (glow, "vmem"), (rho_panel, "vmem"),
        (local, "vmem"), (received, "vmem"), *touched,
    ]
    aliases = None
    if results is not None:
        aliases = {len(operands) + i: i for i in range(2)}
        operands += [(result, "any") for result in results]
    return call(
        functools.partial(finish_kernel, first, starts, results is not None),
        "finish", operands,
        [(out_shape, F32, "any"), (rho_panel.shape, F32, "any")], after,
        scratch=[
            pltpu.VMEM((2, rows, 2 * width), F32),
            pltpu.VMEM((2, rows, 2 * width), F32),
            pltpu.VMEM((poles, 2, rows, width), F32),
            pltpu.SemaphoreType.DMA((poles + 1,)),
        ],
        aliases=aliases,
        cost=cost,
    )


def per_device(
    aux_modes,
    rho_panel,
    ham_blocks,
    block_counts,
    block_offsets,
    lead_gamma,
    pole_energy,
    residues,
    pole_lead,
):
    poles, _, rows, width = aux_modes.shape
    nblock = rows // width
    halo = REACH * width
    devices = lax.axis_size("row")
    odd = (lax.axis_index("row") % 2).astype(jnp.int32).reshape(1)
    count = lax.axis_size("pole")
    me = lax.axis_index("pole")
    inner = count // 2 - 1
    line = count % 2 == 0 and count >= 4

    taken = ((me == 0) | (me == count - 1)).astype(jnp.int32).reshape(1)
    sends = taken if line else jnp.ones_like(taken)

    chunks = CHUNKS
    ranges = [(c * rows // chunks, (c + 1) * rows // chunks) for c in range(chunks)]
    ranges = [ranges[1], ranges[0], *ranges[2:]]
    sizes = [b - a for a, b in ranges]

    (part,), token = call(
        functools.partial(first_kernel, *ranges[0]), "mix",
        [(sends, "smem"), (pole_lead, "smem"), (residues, "smem"), (aux_modes, "hbm")],
        [((2, sizes[0], 2 * width), F32, "vmem")],
        scratch=[pltpu.VMEM((poles, 2, sizes[0], width), F32), pltpu.SemaphoreType.DMA((4,))],
    )
    later, token = call(
        functools.partial(later_kernel, ranges), "mix_later",
        [(pole_lead, "smem"), (residues, "smem"), (odd, "smem"), (lead_gamma, "vmem"), (aux_modes, "hbm")],
        [((2, size, 2 * width), F32, "vmem") for size in sizes]
        + [((poles, 2, halo, width), F32, "hbm")] * 2
        + [((2, 2 * width, 2 * width), BF16, "vmem")] * 2,
        [token],
        scratch=[
            pltpu.VMEM(aux_modes.shape, F32),
            pltpu.SemaphoreType.DMA((chunks,)),
            pltpu.SemaphoreType.DMA((2,)),
        ],
        limit=8,
    )
    near_edge, far_edge, ghigh, glow = later[chunks:]
    locals_ = later[:chunks]

    near_pairs = [(i, i + 1) for i in range(0, devices - 1, 2)]
    far_pairs = [(i, i + 1) for i in range(1, devices - 1, 2)]
    received = [None] * chunks

    def fold_pairs(stage):
        if stage < inner:
            return [(stage, stage + 1), (count - 1 - stage, count - 2 - stage)]
        if stage == inner:
            return [(inner, inner + 1), (inner + 1, inner)]
        j = 2 * inner + 1 - stage
        return [(j, j - 1), (count - 1 - j, count - j)]

    def send(c, stage):
        if line:
            mine = part if c == stage == 0 else locals_[c]
            received[c] = lax.ppermute(mine, "pole", fold_pairs(stage))
        else:
            received[c] = lax.psum(locals_[c], "pole")

    def take(c, stage):
        nonlocal token
        if stage <= inner:
            (locals_[c],), token = call(
                add_kernel, "add", [(locals_[c], "vmem"), (received[c], "vmem")],
                [(locals_[c].shape, F32, "vmem")], [token], cost=COSTS.get(("add", c, stage), 0),
            )
        else:
            j = 2 * inner + 1 - stage
            target = (me == j - 1) | (me == count - j)
            locals_[c] = jnp.where(target, received[c], locals_[c])

    slopes = [None] * 3
    results = None
    pieces = [(i * nblock // 3, (i + 1) * nblock // 3) for i in range(3)]
    near = far = None

    def work(piece):
        nonlocal token
        slopes[piece], token = ham_part(
            *pieces[piece], aux_modes, ham_blocks, block_counts, block_offsets, pole_energy,
            [token], COSTS.get(("ham", piece), 0),
        )

    def neighbours():
        nonlocal near, far, token
        (near, far), token = call(
            lambda: None, "pass", [], [], [token], through=[(near_edge, "hbm"), (far_edge, "hbm")],
            cost=COSTS.get(("pass",), 0),
        )
        near = lax.ppermute(near, "row", near_pairs + [(b, a) for a, b in near_pairs])
        far = lax.ppermute(far, "row", far_pairs + [(b, a) for a, b in far_pairs])

    def reach():
        nonlocal slopes, token
        slopes, token = edge_part(
            slopes, pieces, near, far, odd, ham_blocks, block_counts, block_offsets, [token]
        )

    def finish(c):
        nonlocal results, token
        local = locals_[c] if line else received[c]
        results, token = finish_rows(
            ranges[c][0], slopes, pieces, local, received[c], taken, rho_panel, ghigh, glow, pole_lead,
            results, aux_modes.shape, [token], COSTS.get(("finish", c), 0),
        )

    for c in range(chunks):
        send(c, 0)
    for step in make_plan(line, 2 * inner, len(pieces)):
        if step[0] == "ham":
            work(step[1])
        elif step[0] == "edge":
            reach()
        elif step[0] == "pass":
            neighbours()
        elif step[0] == "finish":
            finish(step[1])
        else:
            take(*step)
            send(step[0], step[1] + 1)
    return tuple(results)


def make_plan(line, stages, pieces):
    work = [("ham", i) for i in [1, 0, *range(2, pieces)]]
    ending = [("edge",)] + [("finish", c) for c in range(1, CHUNKS)]
    plan = [work.pop(0)]
    if not line:
        return plan + [("pass",)] + work + [("finish", 0)] + ending
    for turn in range(CHUNKS + stages - 1):
        for stage in range(stages):
            if 0 <= turn - stage < CHUNKS:
                plan.append((turn - stage, stage))
            if turn == stage == 0:
                plan.append(("pass",))
        if turn == CHUNKS - 1:
            plan.append(("finish", 0))
        if turn > 0 and work:
            plan.append(work.pop(0))
    return plan + work + ending


def solution(mesh):
    placed = (
        P(("grp", "pole"), None, "row", None),
        P(None, ("grp", "row"), None),
        P(("grp", "row"), None, None, None, None),
        P(("grp", "row")),
        P(("grp", "row"), None),
        P(),
        P(None, ("grp", "pole")),
        P(None, ("grp", "pole")),
        P(("grp", "pole")),
    )
    return jax.shard_map(
        per_device,
        mesh=mesh,
        in_specs=placed,
        out_specs=(P(("grp", "pole"), None, "row", None), P(None, ("grp", "row"), None)),
        check_vma=False,
    )
```

```python
import functools

import jax
import jax.numpy as jnp
from jax import lax
from jax.experimental import pallas as pl
from jax.experimental.pallas import tpu as pltpu
from jax.sharding import PartitionSpec as P

REACH = 2
CHUNKS = 3
F32 = jnp.float32
BF16 = jnp.bfloat16
MIB = 2**20
LIMIT = 6
BIG = 10**10
COSTS = {("add", 1, 0): BIG, ("finish", 0): BIG}
SMEM_SPEC = pl.BlockSpec(memory_space=pltpu.SMEM)
VMEM_SPEC = pl.BlockSpec(memory_space=pltpu.VMEM)
ANY_SPEC = pl.BlockSpec(memory_space=pl.ANY)


def dot(left, right):
    return jnp.dot(left, right, preferred_element_type=F32)


def split_high_low(value):
    high = value.astype(BF16)
    return high, (value - high.astype(F32)).astype(BF16)


def kept(value, place):
    spaces = {"vmem": pltpu.VMEM, "hbm": pltpu.HBM, "smem": pltpu.HBM}
    return pltpu.with_memory_space_constraint(value, spaces[place]) if place in spaces else value


def call(kernel, name, operands, outputs, after=(), scratch=(), aliases=None, through=(), cost=0, limit=LIMIT):
    places = {"smem": SMEM_SPEC, "vmem": VMEM_SPEC, "any": ANY_SPEC, "hbm": ANY_SPEC}
    arrays = [kept(a, place) for a, place in operands]
    passed = [kept(a, place) for a, place in through]
    specs = [places[place] for _, place in operands]
    count = len(operands)
    skipped = len(through) + len(after)
    aliases = dict(aliases or {})
    for i in range(len(through)):
        aliases[count + i] = len(outputs) + i

    def body(*refs):
        refs, outs = refs[:count], refs[count + skipped :]
        kernel(*refs, *outs[: len(outputs)], *outs[len(outputs) + len(through) + 1 :])

    shapes = [
        {"vmem": pltpu.VMEM, "hbm": pltpu.HBM}.get(place, jax.ShapeDtypeStruct)(shape, dtype)
        for shape, dtype, place in [*outputs, *((a.shape, a.dtype, place) for a, place in through)]
    ]
    result = pl.pallas_call(
        body,
        in_specs=specs + [places[place] for _, place in through] + [ANY_SPEC] * len(after),
        out_specs=[places[place] for _, _, place in outputs] + [places[place] for _, place in through] + [ANY_SPEC],
        out_shape=shapes + [jax.ShapeDtypeStruct((8, 128), F32)],
        scratch_shapes=list(scratch),
        input_output_aliases=aliases,
        compiler_params=pltpu.CompilerParams(vmem_limit_bytes=limit * MIB),
        cost_estimate=pl.CostEstimate(flops=cost, bytes_accessed=cost, transcendentals=0),
        name=name,
    )(*arrays, *passed, *after)
    return list(result[:-1]), result[-1]


def mix_tile(lead_ref, residue_ref, load, store, poles, width):
    sums = [None] * 4
    for pole in range(poles):
        real, imag = load(pole)
        for lead in range(2):
            alive = (lead_ref[pole] == lead).astype(F32)
            coef_real = alive * residue_ref[0, pole]
            coef_imag = alive * residue_ref[1, pole]
            terms = (
                coef_real * real - coef_imag * imag,
                coef_real * imag + coef_imag * real,
            )
            for part in range(2):
                slot = 2 * part + lead
                sums[slot] = terms[part] if pole == 0 else sums[slot] + terms[part]
    for part in range(2):
        for lead in range(2):
            store(part, slice(lead * width, (lead + 1) * width), sums[2 * part + lead])


def mix_range(lead_ref, residue_ref, aux_ref, out_ref, aux_start, out_start, rows, tile=32):
    poles = aux_ref.shape[0]
    width = aux_ref.shape[-1]
    tile = next(t for t in (tile, 16, 8) if rows % t == 0)

    def step(i, carry):
        at = pl.ds(pl.multiple_of(aux_start + i * tile, 8), tile)
        to = pl.ds(pl.multiple_of(out_start + i * tile, 8), tile)

        def load(pole):
            return aux_ref[pole, 0, at, :], aux_ref[pole, 1, at, :]

        def store(part, columns, value):
            out_ref[part, to, columns] = value

        mix_tile(lead_ref, residue_ref, load, store, poles, width)
        return carry

    lax.fori_loop(0, rows // tile, step, 0)


def first_kernel(first, last, axis, lead_ref, residue_ref, aux_ref, out_ref, mode_ref, lead_here, residue_here, sems, scalar_sems):
    pieces = 4
    size = (last - first) // pieces
    copies = [
        pltpu.make_async_copy(
            aux_ref.at[:, :, pl.ds(first + i * size, size), :],
            mode_ref.at[:, :, pl.ds(i * size, size), :],
            sems.at[i],
        )
        for i in range(pieces)
    ]
    scalars = [
        pltpu.make_async_copy(lead_ref, lead_here, scalar_sems.at[0]),
        pltpu.make_async_copy(residue_ref, residue_here, scalar_sems.at[1]),
    ]

    def work():
        for copy in scalars + copies:
            copy.start()
        for copy in scalars:
            copy.wait()
        for i, copy in enumerate(copies):
            copy.wait()
            mix_range(lead_here, residue_here, mode_ref, out_ref, i * size, i * size, size)

    if axis is None:
        work()
    else:
        me = lax.axis_index(axis)
        pl.when((me == 0) | (me == lax.axis_size(axis) - 1))(work)


def later_kernel(ranges, lead_ref, residue_ref, odd_ref, gamma_ref, aux_ref, *rest):
    outs = rest[: len(ranges)]
    near_ref, far_ref, ghigh_ref, glow_ref, mode_ref, sems, edge_sems = rest[len(ranges) :]
    rows = aux_ref.shape[2]
    halo = near_ref.shape[2]
    copies = []
    place = 0
    places = []
    for i, (first, last) in enumerate(ranges):
        at = pl.ds(first, last - first)
        to = pl.ds(place, last - first)
        copies.append(pltpu.make_async_copy(aux_ref.at[:, :, at, :], mode_ref.at[:, :, to, :], sems.at[i]))
        places.append(place)
        place += last - first
    order = [*range(1, len(ranges)), 0]
    for i in order:
        copies[i].start()
    for lead in range(2):
        gamma_real = gamma_ref[lead, 0]
        gamma_imag = gamma_ref[lead, 1]
        gamma = jnp.concatenate(
            [
                jnp.concatenate([gamma_real, gamma_imag], axis=1),
                jnp.concatenate([-gamma_imag, gamma_real], axis=1),
            ],
            axis=0,
        )
        ghigh_ref[lead], glow_ref[lead] = split_high_low(gamma)
    odd = odd_ref[0]
    held = [(0, halo), (rows - halo, rows)]
    whole = all(side in ranges for side in held)
    sides = ((0, 1 - odd), (rows - halo, odd))
    edges = []
    for i, (start, side) in enumerate(sides):
        if whole:
            copies[ranges.index(held[i])].wait()
            source = mode_ref.at[:, :, pl.ds(places[ranges.index(held[i])], halo), :]
        else:
            source = aux_ref.at[:, :, pl.ds(start, halo), :]
        for j, ref in enumerate((near_ref, far_ref)):
            edge = pltpu.make_async_copy(source, ref, edge_sems.at[j])
            pl.when(side == j)(edge.start)
        edges.append(pltpu.make_async_copy(source, near_ref, edge_sems.at[i]))
    for i in order:
        first, last = ranges[i]
        if not (whole and ranges[i] in held):
            copies[i].wait()
        mix_range(lead_ref, residue_ref, mode_ref, outs[i], places[i], 0, last - first)
    for edge in edges:
        edge.wait()


def add_kernel(left_ref, right_ref, out_ref):
    out_ref[...] = left_ref[...] + right_ref[...]


def pair_split(ham_ref, index, which):
    ham_real = ham_ref[index, which, 0]
    ham_imag = ham_ref[index, which, 1]
    pair = jnp.concatenate(
        [
            jnp.concatenate([ham_real, -ham_imag], axis=1),
            jnp.concatenate([ham_imag, ham_real], axis=1),
        ],
        axis=0,
    )
    return split_high_low(pair)


def product(ham_ref, index, which, mode_ref, place, rows, high_ref, low_ref):
    poles = mode_ref.shape[-4]
    width = mode_ref.shape[-1]
    for pole in range(poles):
        for part in range(2):
            high, low = split_high_low(mode_ref[place, pole, part, rows, :])
            where = (pl.ds(part * width, width), pl.ds(pole * width, width))
            high_ref[where] = high
            low_ref[where] = low
    pair_high, pair_low = pair_split(ham_ref, index, which)
    return dot(pair_high, high_ref[...]) + dot(pair_high, low_ref[...]) + dot(pair_low, high_ref[...])


def ham_kernel(first, last, count_ref, offset_ref, energy_ref, ham_ref, aux_ref, out_ref, blocks_ref, mode_ref, high_ref, low_ref, total_ref, ham_sems, mode_sems):
    poles, _, rows, width = aux_ref.shape
    nblock = rows // width
    slots = ham_ref.shape[1]
    base = max(first - REACH, 0)
    ending = min(last + REACH, nblock)
    own = range(first, last)
    others = [block for block in range(base, ending) if block not in own]
    heads = []
    tails = []
    for i, row in enumerate(own):
        heads.append(pltpu.make_async_copy(ham_ref.at[row, 0], blocks_ref.at[i, 0], ham_sems.at[i, 0]))
        rest = pl.ds(1, slots - 1)
        tails.append(pltpu.make_async_copy(ham_ref.at[row, rest], blocks_ref.at[i, rest], ham_sems.at[i, 1]))
    mode_copies = {
        block: pltpu.make_async_copy(
            aux_ref.at[:, :, pl.ds(block * width, width), :], mode_ref.at[block - base], mode_sems.at[block - base]
        )
        for block in range(base, ending)
    }
    for i, row in enumerate(own):
        heads[i].start()
        mode_copies[row].start()
    for i, row in enumerate(own):
        pl.when(count_ref[row] > 1)(tails[i].start)
    needed = {}
    for block in others:
        uses = [
            (which < count_ref[row]) & (row + offset_ref[row, which] == block)
            for row in own
            for which in range(1, slots)
        ]
        needed[block] = functools.reduce(jnp.logical_or, uses)
        pl.when(needed[block])(mode_copies[block].start)
    whole = pl.ds(0, width)
    for i, row in enumerate(own):
        heads[i].wait()
        mode_copies[row].wait()
        total_ref[i] = product(blocks_ref, i, 0, mode_ref, row - base, whole, high_ref, low_ref)
    for i, row in enumerate(own):
        pl.when(count_ref[row] > 1)(tails[i].wait)
    for block in others:
        pl.when(needed[block])(mode_copies[block].wait)
    for i, row in enumerate(own):

        def slot(which, carry):
            place = row + offset_ref[row, which]

            @pl.when((place >= 0) & (place < nblock))
            def _():
                total_ref[i] += product(blocks_ref, i, which, mode_ref, place - base, whole, high_ref, low_ref)

            return carry

        lax.fori_loop(1, count_ref[row], slot, 0)
        for pole in range(poles):
            real = mode_ref[row - base, pole, 0]
            imag = mode_ref[row - base, pole, 1]
            energy_real = energy_ref[0, pole]
            energy_imag = energy_ref[1, pole]
            columns = slice(pole * width, (pole + 1) * width)
            at = pl.ds(i * width, width)
            out_ref[pole, 0, at, :] = total_ref[i, width:, columns] - (energy_real * imag + energy_imag * real)
            out_ref[pole, 1, at, :] = (energy_real * real - energy_imag * imag) - total_ref[i, :width, columns]


def ham_part(first, last, aux_modes, ham_blocks, block_counts, block_offsets, pole_energy, after, cost):
    poles, _, rows, width = aux_modes.shape
    nblock, slots = ham_blocks.shape[:2]
    n = last - first
    held = min(last + REACH, nblock) - max(first - REACH, 0)
    (slopes,), token = call(
        functools.partial(ham_kernel, first, last),
        "ham",
        [
            (block_counts, "smem"), (block_offsets, "smem"), (pole_energy, "smem"),
            (ham_blocks, "hbm"), (aux_modes, "hbm"),
        ],
        [((poles, 2, n * width, width), F32, "vmem")], after,
        scratch=[
            pltpu.VMEM((n, slots, 2, width, width), F32),
            pltpu.VMEM((held, poles, 2, width, width), F32),
            pltpu.VMEM((2 * width, poles * width), BF16),
            pltpu.VMEM((2 * width, poles * width), BF16),
            pltpu.VMEM((n, 2 * width, poles * width), F32),
            pltpu.SemaphoreType.DMA((n, 2)),
            pltpu.SemaphoreType.DMA((held,)),
        ],
        cost=cost,
        limit=14,
    )
    return slopes, token


def edge_kernel(nblock, bounds, count_ref, offset_ref, odd_ref, ham_ref, near_ref, far_ref, *refs):
    pieces = len(bounds)
    ins, outs = refs[:pieces], refs[pieces : 2 * pieces]
    blocks_ref, high_ref, low_ref, total_ref, ham_sems = refs[2 * pieces :]
    poles = near_ref.shape[1]
    width = near_ref.shape[-1]
    odd = odd_ref[0]
    edge_rows = list(range(REACH)) + list(range(nblock - REACH, nblock))
    ham_copies = [
        pltpu.make_async_copy(ham_ref.at[row], blocks_ref.at[i], ham_sems.at[i]) for i, row in enumerate(edge_rows)
    ]
    for copy in ham_copies:
        copy.start()
    for in_ref, out_ref in zip(ins, outs):
        out_ref[...] = in_ref[...]
    for i, row in enumerate(edge_rows):
        out_ref, at = next(
            (ref, pl.ds((row - a) * width, width)) for ref, (a, b) in zip(outs, bounds) if a <= row < b
        )
        ham_copies[i].wait()

        def slot(which, carry):
            place = row + offset_ref[row, which]
            below = place < 0
            above = place >= nblock
            start = pl.multiple_of(jnp.where(below, place + REACH, place - nblock) * width, width)

            def add(halo_ref):
                total_ref[...] = product(blocks_ref, i, which, halo_ref, 0, pl.ds(start, width), high_ref, low_ref)
                for pole in range(poles):
                    columns = slice(pole * width, (pole + 1) * width)
                    out_ref[pole, 0, at, :] += total_ref[width:, columns]
                    out_ref[pole, 1, at, :] -= total_ref[:width, columns]

            pl.when((below & (odd == 1)) | (above & (odd == 0)))(lambda: add(near_ref))
            pl.when((below & (odd == 0)) | (above & (odd == 1)))(lambda: add(far_ref))
            return carry

        lax.fori_loop(1, count_ref[row], slot, 0)


def edge_part(slopes, bounds, near, far, odd, ham_blocks, block_counts, block_offsets, after):
    nblock, slots = ham_blocks.shape[:2]
    poles, _, _, width = near.shape
    reached = [i for i, (a, b) in enumerate(bounds) if a < REACH or b > nblock - REACH]
    outs, token = call(
        functools.partial(edge_kernel, nblock, [bounds[i] for i in reached]), "edge",
        [
            (block_counts, "smem"), (block_offsets, "smem"), (odd, "smem"), (ham_blocks, "hbm"),
            (near[None], "vmem"), (far[None], "vmem"),
        ]
        + [(slopes[i], "vmem") for i in reached],
        [(slopes[i].shape, F32, "vmem") for i in reached], after,
        scratch=[
            pltpu.VMEM((2 * REACH, slots, 2, width, width), F32),
            pltpu.VMEM((2 * width, poles * width), BF16),
            pltpu.VMEM((2 * width, poles * width), BF16),
            pltpu.VMEM((2 * width, poles * width), F32),
            pltpu.SemaphoreType.DMA((2 * REACH,)),
        ],
        limit=8,
    )
    slopes = list(slopes)
    for i, out in zip(reached, outs):
        slopes[i] = out
    return slopes, token


def finish_kernel(first, starts, chained, *refs):
    lead_ref, taken_ref, ghigh_ref, glow_ref, rho_ref, local_ref, received_ref = refs[:7]
    slope_refs = refs[7 : 7 + len(starts)]
    refs = refs[7 + len(starts) + (2 if chained else 0) :]
    out_ref, lead_out_ref, wide_ref, source_ref, panel_ref, sems = refs
    poles, _, _, width = slope_refs[0].shape
    rows = local_ref.shape[1]
    at = pl.ds(first, rows)
    lead_term = jnp.where(taken_ref[0] == 1, received_ref[...], local_ref[...])
    wide_ref[...] = lead_term
    copies = [pltpu.make_async_copy(wide_ref, lead_out_ref.at[:, at, :], sems.at[poles])]
    copies[0].start()
    for lead in range(2):
        columns = slice(lead * width, (lead + 1) * width)
        pair = jnp.concatenate(
            [
                rho_ref[part, at, columns] + 0.25 * wide_ref[part, :, columns]
                for part in range(2)
            ],
            axis=1,
        )
        high, low = split_high_low(pair)
        source_ref[lead] = (
            dot(high, ghigh_ref[lead]) + dot(high, glow_ref[lead]) + dot(low, ghigh_ref[lead])
        )
    for pole in range(poles):
        lead = lead_ref[pole]
        for slope_ref, start in zip(slope_refs, starts):
            low_row = max(start, first)
            high_row = min(start + slope_ref.shape[2], first + rows)
            from_ = pl.ds(low_row - start, high_row - low_row)
            to = pl.ds(low_row - first, high_row - low_row)
            panel_ref[pole, 0, to, :] = slope_ref[pole, 0, from_, :] + source_ref[lead, to, width:]
            panel_ref[pole, 1, to, :] = slope_ref[pole, 1, from_, :] - source_ref[lead, to, :width]
        copies.append(
            pltpu.make_async_copy(panel_ref.at[pole], out_ref.at[pole, :, at, :], sems.at[pole])
        )
        copies[-1].start()
    for copy in copies:
        copy.wait()


def finish_rows(
    first, slopes, pieces, local, received, taken, rho_panel, ghigh, glow, pole_lead, results, out_shape, after, cost
):
    poles, _, _, width = out_shape
    rows = local.shape[1]
    starts = []
    touched = []
    for piece, (a, b) in zip(slopes, pieces):
        if a * width < first + rows and b * width > first:
            starts.append(a * width)
            touched.append((piece, "vmem"))
    operands = [
        (pole_lead, "smem"), (taken, "smem"), (ghigh, "vmem"), (glow, "vmem"), (rho_panel, "vmem"),
        (local, "vmem"), (received, "vmem"), *touched,
    ]
    aliases = None
    if results is not None:
        aliases = {len(operands) + i: i for i in range(2)}
        operands += [(result, "any") for result in results]
    return call(
        functools.partial(finish_kernel, first, starts, results is not None),
        "finish", operands,
        [(out_shape, F32, "any"), (rho_panel.shape, F32, "any")], after,
        scratch=[
            pltpu.VMEM((2, rows, 2 * width), F32),
            pltpu.VMEM((2, rows, 2 * width), F32),
            pltpu.VMEM((poles, 2, rows, width), F32),
            pltpu.SemaphoreType.DMA((poles + 1,)),
        ],
        aliases=aliases,
        cost=cost,
    )


def per_device(
    aux_modes,
    rho_panel,
    ham_blocks,
    block_counts,
    block_offsets,
    lead_gamma,
    pole_energy,
    residues,
    pole_lead,
):
    poles, _, rows, width = aux_modes.shape
    nblock = rows // width
    halo = REACH * width
    devices = lax.axis_size("row")
    odd = (lax.axis_index("row") % 2).astype(jnp.int32).reshape(1)
    count = lax.axis_size("pole")
    me = lax.axis_index("pole")
    inner = count // 2 - 1
    line = count % 2 == 0 and count >= 4

    taken = ((me == 0) | (me == count - 1)).astype(jnp.int32).reshape(1)

    sends = taken if line else jnp.ones_like(taken)

    chunks = CHUNKS
    ranges = [(c * rows // chunks, (c + 1) * rows // chunks) for c in range(chunks)]
    ranges = [ranges[1], ranges[0], *ranges[2:]]
    sizes = [b - a for a, b in ranges]

    (part,), token = call(
        functools.partial(first_kernel, *ranges[0], "pole" if line else None), "mix",
        [(pole_lead, "hbm"), (residues, "hbm"), (aux_modes, "hbm")],
        [((2, sizes[0], 2 * width), F32, "vmem")], [sends],
        scratch=[
            pltpu.VMEM((poles, 2, sizes[0], width), F32),
            pltpu.SMEM(pole_lead.shape, jnp.int32),
            pltpu.SMEM(residues.shape, F32),
            pltpu.SemaphoreType.DMA((4,)),
            pltpu.SemaphoreType.DMA((2,)),
        ],
    )
    later, token = call(
        functools.partial(later_kernel, ranges), "mix_later",
        [(pole_lead, "smem"), (residues, "smem"), (odd, "smem"), (lead_gamma, "vmem"), (aux_modes, "hbm")],
        [((2, size, 2 * width), F32, "vmem") for size in sizes]
        + [((poles, 2, halo, width), F32, "hbm")] * 2
        + [((2, 2 * width, 2 * width), BF16, "vmem")] * 2,
        [token],
        scratch=[
            pltpu.VMEM(aux_modes.shape, F32),
            pltpu.SemaphoreType.DMA((chunks,)),
            pltpu.SemaphoreType.DMA((2,)),
        ],
        limit=8,
    )
    near_edge, far_edge, ghigh, glow = later[chunks:]
    locals_ = later[:chunks]

    near_pairs = [(i, i + 1) for i in range(0, devices - 1, 2)]
    far_pairs = [(i, i + 1) for i in range(1, devices - 1, 2)]
    received = [None] * chunks

    def fold_pairs(stage):
        if stage < inner:
            return [(stage, stage + 1), (count - 1 - stage, count - 2 - stage)]
        if stage == inner:
            return [(inner, inner + 1), (inner + 1, inner)]
        j = 2 * inner + 1 - stage
        return [(j, j - 1), (count - 1 - j, count - j)]

    def send(c, stage):
        if line:
            mine = part if c == stage == 0 else locals_[c]
            received[c] = lax.ppermute(mine, "pole", fold_pairs(stage))
        else:
            received[c] = lax.psum(locals_[c], "pole")

    def take(c, stage):
        nonlocal token
        if stage <= inner:
            (locals_[c],), token = call(
                add_kernel, "add", [(locals_[c], "vmem"), (received[c], "vmem")],
                [(locals_[c].shape, F32, "vmem")], [token], cost=COSTS.get(("add", c, stage), 0),
            )
        else:
            j = 2 * inner + 1 - stage
            target = (me == j - 1) | (me == count - j)
            locals_[c] = jnp.where(target, received[c], locals_[c])

    slopes = [None] * 3
    results = None
    pieces = [(i * nblock // 3, (i + 1) * nblock // 3) for i in range(3)]
    near = far = None

    def work(piece):
        nonlocal token
        slopes[piece], token = ham_part(
            *pieces[piece], aux_modes, ham_blocks, block_counts, block_offsets, pole_energy,
            [token], COSTS.get(("ham", piece), 0),
        )

    def neighbours():
        nonlocal near, far, token
        (near, far), token = call(
            lambda: None, "pass", [], [], [token], through=[(near_edge, "hbm"), (far_edge, "hbm")],
            cost=COSTS.get(("pass",), 0),
        )
        near = lax.ppermute(near, "row", near_pairs + [(b, a) for a, b in near_pairs])
        far = lax.ppermute(far, "row", far_pairs + [(b, a) for a, b in far_pairs])

    def reach():
        nonlocal slopes, token
        slopes, token = edge_part(
            slopes, pieces, near, far, odd, ham_blocks, block_counts, block_offsets, [token]
        )

    def finish(c):
        nonlocal results, token
        local = locals_[c] if line else received[c]
        results, token = finish_rows(
            ranges[c][0], slopes, pieces, local, received[c], taken, rho_panel, ghigh, glow, pole_lead,
            results, aux_modes.shape, [token], COSTS.get(("finish", c), 0),
        )

    for c in range(chunks):
        send(c, 0)
    for step in make_plan(line, 2 * inner, len(pieces)):
        if step[0] == "ham":
            work(step[1])
        elif step[0] == "edge":
            reach()
        elif step[0] == "pass":
            neighbours()
        elif step[0] == "finish":
            finish(step[1])
        else:
            take(*step)
            send(step[0], step[1] + 1)
    return tuple(results)


def make_plan(line, stages, pieces):
    work = [("ham", i) for i in [1, 0, *range(2, pieces)]]
    ending = [("edge",)] + [("finish", c) for c in range(1, CHUNKS)]
    plan = [work.pop(0)]
    if not line:
        return plan + [("pass",)] + work + [("finish", 0)] + ending
    for turn in range(CHUNKS + stages - 1):
        for stage in range(stages):
            if 0 <= turn - stage < CHUNKS:
                plan.append((turn - stage, stage))
            if turn == stage == 0:
                plan.append(("pass",))
        if turn == CHUNKS - 1:
            plan.append(("finish", 0))
        if turn > 0 and work:
            plan.append(work.pop(0))
    return plan + work + ending


def solution(mesh):
    placed = (
        P(("grp", "pole"), None, "row", None),
        P(None, ("grp", "row"), None),
        P(("grp", "row"), None, None, None, None),
        P(("grp", "row")),
        P(("grp", "row"), None),
        P(),
        P(None, ("grp", "pole")),
        P(None, ("grp", "pole")),
        P(("grp", "pole")),
    )
    return jax.shard_map(
        per_device,
        mesh=mesh,
        in_specs=placed,
        out_specs=(P(("grp", "pole"), None, "row", None), P(None, ("grp", "row"), None)),
        check_vma=False,
    )
```

```python
import functools

import jax
import jax.numpy as jnp
from jax import lax
from jax.experimental import pallas as pl
from jax.experimental.pallas import tpu as pltpu
from jax.sharding import PartitionSpec as P

REACH = 2
CHUNKS = 3
F32 = jnp.float32
BF16 = jnp.bfloat16
MIB = 2**20
LIMIT = 6
BIG = 10**10
COSTS = {("add", 1, 0): BIG, ("finish", 0): BIG}
SMEM_SPEC = pl.BlockSpec(memory_space=pltpu.SMEM)
VMEM_SPEC = pl.BlockSpec(memory_space=pltpu.VMEM)
ANY_SPEC = pl.BlockSpec(memory_space=pl.ANY)


def dot(left, right):
    return jnp.dot(left, right, preferred_element_type=F32)


def split_high_low(value):
    high = value.astype(BF16)
    return high, (value - high.astype(F32)).astype(BF16)


def kept(value, place):
    spaces = {"vmem": pltpu.VMEM, "hbm": pltpu.HBM, "smem": pltpu.HBM}
    return pltpu.with_memory_space_constraint(value, spaces[place]) if place in spaces else value


def call(kernel, name, operands, outputs, after=(), scratch=(), aliases=None, through=(), cost=0, limit=LIMIT):
    places = {"smem": SMEM_SPEC, "vmem": VMEM_SPEC, "any": ANY_SPEC, "hbm": ANY_SPEC}
    arrays = [kept(a, place) for a, place in operands]
    passed = [kept(a, place) for a, place in through]
    specs = [places[place] for _, place in operands]
    count = len(operands)
    skipped = len(through) + len(after)
    aliases = dict(aliases or {})
    for i in range(len(through)):
        aliases[count + i] = len(outputs) + i

    def body(*refs):
        refs, outs = refs[:count], refs[count + skipped :]
        kernel(*refs, *outs[: len(outputs)], *outs[len(outputs) + len(through) + 1 :])

    shapes = [
        {"vmem": pltpu.VMEM, "hbm": pltpu.HBM}.get(place, jax.ShapeDtypeStruct)(shape, dtype)
        for shape, dtype, place in [*outputs, *((a.shape, a.dtype, place) for a, place in through)]
    ]
    result = pl.pallas_call(
        body,
        in_specs=specs + [places[place] for _, place in through] + [ANY_SPEC] * len(after),
        out_specs=[places[place] for _, _, place in outputs] + [places[place] for _, place in through] + [ANY_SPEC],
        out_shape=shapes + [jax.ShapeDtypeStruct((8, 128), F32)],
        scratch_shapes=list(scratch),
        input_output_aliases=aliases,
        compiler_params=pltpu.CompilerParams(vmem_limit_bytes=limit * MIB),
        cost_estimate=pl.CostEstimate(flops=cost, bytes_accessed=cost, transcendentals=0),
        name=name,
    )(*arrays, *passed, *after)
    return list(result[:-1]), result[-1]


def mix_tile(lead_ref, residue_ref, load, store, poles, width):
    sums = [None] * 4
    for pole in range(poles):
        real, imag = load(pole)
        for lead in range(2):
            alive = (lead_ref[pole] == lead).astype(F32)
            coef_real = alive * residue_ref[0, pole]
            coef_imag = alive * residue_ref[1, pole]
            terms = (
                coef_real * real - coef_imag * imag,
                coef_real * imag + coef_imag * real,
            )
            for part in range(2):
                slot = 2 * part + lead
                sums[slot] = terms[part] if pole == 0 else sums[slot] + terms[part]
    for part in range(2):
        for lead in range(2):
            store(part, slice(lead * width, (lead + 1) * width), sums[2 * part + lead])


def mix_range(lead_ref, residue_ref, aux_ref, out_ref, aux_start, out_start, rows, tile=32):
    poles = aux_ref.shape[0]
    width = aux_ref.shape[-1]
    tile = next(t for t in (tile, 16, 8) if rows % t == 0)

    def step(i, carry):
        at = pl.ds(pl.multiple_of(aux_start + i * tile, 8), tile)
        to = pl.ds(pl.multiple_of(out_start + i * tile, 8), tile)

        def load(pole):
            return aux_ref[pole, 0, at, :], aux_ref[pole, 1, at, :]

        def store(part, columns, value):
            out_ref[part, to, columns] = value

        mix_tile(lead_ref, residue_ref, load, store, poles, width)
        return carry

    lax.fori_loop(0, rows // tile, step, 0)


def first_kernel(first, last, axis, lead_ref, residue_ref, aux_ref, out_ref, mode_ref, lead_here, residue_here, sems, scalar_sems):
    pieces = 4
    size = (last - first) // pieces
    copies = [
        pltpu.make_async_copy(
            aux_ref.at[:, :, pl.ds(first + i * size, size), :],
            mode_ref.at[:, :, pl.ds(i * size, size), :],
            sems.at[i],
        )
        for i in range(pieces)
    ]
    scalars = [
        pltpu.make_async_copy(lead_ref, lead_here, scalar_sems.at[0]),
        pltpu.make_async_copy(residue_ref, residue_here, scalar_sems.at[1]),
    ]

    def work():
        for copy in scalars + copies:
            copy.start()
        for copy in scalars:
            copy.wait()
        for i, copy in enumerate(copies):
            copy.wait()
            mix_range(lead_here, residue_here, mode_ref, out_ref, i * size, i * size, size)

    if axis is None:
        work()
    else:
        me = lax.axis_index(axis)
        pl.when((me == 0) | (me == lax.axis_size(axis) - 1))(work)


def later_kernel(ranges, lead_ref, residue_ref, odd_ref, gamma_ref, aux_ref, *rest):
    outs = rest[: len(ranges)]
    near_ref, far_ref, ghigh_ref, glow_ref, mode_ref, sems, edge_sems = rest[len(ranges) :]
    rows = aux_ref.shape[2]
    halo = near_ref.shape[2]
    copies = []
    place = 0
    places = []
    for i, (first, last) in enumerate(ranges):
        at = pl.ds(first, last - first)
        to = pl.ds(place, last - first)
        copies.append(pltpu.make_async_copy(aux_ref.at[:, :, at, :], mode_ref.at[:, :, to, :], sems.at[i]))
        places.append(place)
        place += last - first
    order = [*range(1, len(ranges)), 0]
    for i in order:
        copies[i].start()
    for lead in range(2):
        gamma_real = gamma_ref[lead, 0]
        gamma_imag = gamma_ref[lead, 1]
        gamma = jnp.concatenate(
            [
                jnp.concatenate([gamma_real, gamma_imag], axis=1),
                jnp.concatenate([-gamma_imag, gamma_real], axis=1),
            ],
            axis=0,
        )
        ghigh_ref[lead], glow_ref[lead] = split_high_low(gamma)
    odd = odd_ref[0]
    held = [(0, halo), (rows - halo, rows)]
    whole = all(side in ranges for side in held)
    sides = ((0, 1 - odd), (rows - halo, odd))
    edges = []
    for i, (start, side) in enumerate(sides):
        if whole:
            copies[ranges.index(held[i])].wait()
            source = mode_ref.at[:, :, pl.ds(places[ranges.index(held[i])], halo), :]
        else:
            source = aux_ref.at[:, :, pl.ds(start, halo), :]
        for j, ref in enumerate((near_ref, far_ref)):
            edge = pltpu.make_async_copy(source, ref, edge_sems.at[j])
            pl.when(side == j)(edge.start)
        edges.append(pltpu.make_async_copy(source, near_ref, edge_sems.at[i]))
    for i in order:
        first, last = ranges[i]
        if not (whole and ranges[i] in held):
            copies[i].wait()
        mix_range(lead_ref, residue_ref, mode_ref, outs[i], places[i], 0, last - first)
    for edge in edges:
        edge.wait()


def add_kernel(left_ref, right_ref, out_ref):
    out_ref[...] = left_ref[...] + right_ref[...]


def pair_split(ham_ref, index, which):
    ham_real = ham_ref[index, which, 0]
    ham_imag = ham_ref[index, which, 1]
    pair = jnp.concatenate(
        [
            jnp.concatenate([ham_real, -ham_imag], axis=1),
            jnp.concatenate([ham_imag, ham_real], axis=1),
        ],
        axis=0,
    )
    return split_high_low(pair)


def product(ham_ref, index, which, mode_ref, place, rows, high_ref, low_ref):
    poles = mode_ref.shape[-4]
    width = mode_ref.shape[-1]
    for pole in range(poles):
        for part in range(2):
            high, low = split_high_low(mode_ref[place, pole, part, rows, :])
            where = (pl.ds(part * width, width), pl.ds(pole * width, width))
            high_ref[where] = high
            low_ref[where] = low
    pair_high, pair_low = pair_split(ham_ref, index, which)
    return dot(pair_high, high_ref[...]) + dot(pair_high, low_ref[...]) + dot(pair_low, high_ref[...])


def ham_kernel(first, last, count_ref, offset_ref, energy_ref, ham_ref, aux_ref, out_ref, blocks_ref, mode_ref, high_ref, low_ref, total_ref, ham_sems, mode_sems):
    poles, _, rows, width = aux_ref.shape
    nblock = rows // width
    slots = ham_ref.shape[1]
    base = max(first - REACH, 0)
    ending = min(last + REACH, nblock)
    own = range(first, last)
    others = [block for block in range(base, ending) if block not in own]
    heads = []
    tails = []
    for i, row in enumerate(own):
        heads.append(pltpu.make_async_copy(ham_ref.at[row, 0], blocks_ref.at[i, 0], ham_sems.at[i, 0]))
        rest = pl.ds(1, slots - 1)
        tails.append(pltpu.make_async_copy(ham_ref.at[row, rest], blocks_ref.at[i, rest], ham_sems.at[i, 1]))
    mode_copies = {
        block: pltpu.make_async_copy(
            aux_ref.at[:, :, pl.ds(block * width, width), :], mode_ref.at[block - base], mode_sems.at[block - base]
        )
        for block in range(base, ending)
    }
    for i, row in enumerate(own):
        heads[i].start()
        mode_copies[row].start()
    for i, row in enumerate(own):
        pl.when(count_ref[row] > 1)(tails[i].start)
    needed = {}
    for block in others:
        uses = [
            (which < count_ref[row]) & (row + offset_ref[row, which] == block)
            for row in own
            for which in range(1, slots)
        ]
        needed[block] = functools.reduce(jnp.logical_or, uses)
        pl.when(needed[block])(mode_copies[block].start)
    whole = pl.ds(0, width)
    for i, row in enumerate(own):
        heads[i].wait()
        mode_copies[row].wait()
        total_ref[i] = product(blocks_ref, i, 0, mode_ref, row - base, whole, high_ref, low_ref)
    for i, row in enumerate(own):
        pl.when(count_ref[row] > 1)(tails[i].wait)
    for block in others:
        pl.when(needed[block])(mode_copies[block].wait)
    for i, row in enumerate(own):

        def slot(which, carry):
            place = row + offset_ref[row, which]

            @pl.when((place >= 0) & (place < nblock))
            def _():
                total_ref[i] += product(blocks_ref, i, which, mode_ref, place - base, whole, high_ref, low_ref)

            return carry

        lax.fori_loop(1, count_ref[row], slot, 0)
        for pole in range(poles):
            real = mode_ref[row - base, pole, 0]
            imag = mode_ref[row - base, pole, 1]
            energy_real = energy_ref[0, pole]
            energy_imag = energy_ref[1, pole]
            columns = slice(pole * width, (pole + 1) * width)
            at = pl.ds(i * width, width)
            out_ref[pole, 0, at, :] = total_ref[i, width:, columns] - (energy_real * imag + energy_imag * real)
            out_ref[pole, 1, at, :] = (energy_real * real - energy_imag * imag) - total_ref[i, :width, columns]


def ham_part(first, last, aux_modes, ham_blocks, block_counts, block_offsets, pole_energy, after, cost):
    poles, _, rows, width = aux_modes.shape
    nblock, slots = ham_blocks.shape[:2]
    n = last - first
    held = min(last + REACH, nblock) - max(first - REACH, 0)
    (slopes,), token = call(
        functools.partial(ham_kernel, first, last),
        "ham",
        [
            (block_counts, "smem"), (block_offsets, "smem"), (pole_energy, "smem"),
            (ham_blocks, "hbm"), (aux_modes, "hbm"),
        ],
        [((poles, 2, n * width, width), F32, "vmem")], after,
        scratch=[
            pltpu.VMEM((n, slots, 2, width, width), F32),
            pltpu.VMEM((held, poles, 2, width, width), F32),
            pltpu.VMEM((2 * width, poles * width), BF16),
            pltpu.VMEM((2 * width, poles * width), BF16),
            pltpu.VMEM((n, 2 * width, poles * width), F32),
            pltpu.SemaphoreType.DMA((n, 2)),
            pltpu.SemaphoreType.DMA((held,)),
        ],
        cost=cost,
        limit=14,
    )
    return slopes, token


def edge_kernel(nblock, bounds, count_ref, offset_ref, odd_ref, ham_ref, near_ref, far_ref, *refs):
    pieces = len(bounds)
    ins, outs = refs[:pieces], refs[pieces : 2 * pieces]
    blocks_ref, high_ref, low_ref, total_ref, ham_sems = refs[2 * pieces :]
    poles = near_ref.shape[1]
    width = near_ref.shape[-1]
    odd = odd_ref[0]
    edge_rows = list(range(REACH)) + list(range(nblock - REACH, nblock))
    ham_copies = [
        pltpu.make_async_copy(ham_ref.at[row], blocks_ref.at[i], ham_sems.at[i]) for i, row in enumerate(edge_rows)
    ]
    for copy in ham_copies:
        copy.start()
    for in_ref, out_ref in zip(ins, outs):
        out_ref[...] = in_ref[...]
    for i, row in enumerate(edge_rows):
        out_ref, at = next(
            (ref, pl.ds((row - a) * width, width)) for ref, (a, b) in zip(outs, bounds) if a <= row < b
        )
        ham_copies[i].wait()

        def slot(which, carry):
            place = row + offset_ref[row, which]
            below = place < 0
            above = place >= nblock
            start = pl.multiple_of(jnp.where(below, place + REACH, place - nblock) * width, width)

            def add(halo_ref):
                total_ref[...] = product(blocks_ref, i, which, halo_ref, 0, pl.ds(start, width), high_ref, low_ref)
                for pole in range(poles):
                    columns = slice(pole * width, (pole + 1) * width)
                    out_ref[pole, 0, at, :] += total_ref[width:, columns]
                    out_ref[pole, 1, at, :] -= total_ref[:width, columns]

            pl.when((below & (odd == 1)) | (above & (odd == 0)))(lambda: add(near_ref))
            pl.when((below & (odd == 0)) | (above & (odd == 1)))(lambda: add(far_ref))
            return carry

        lax.fori_loop(1, count_ref[row], slot, 0)


def edge_part(slopes, bounds, near, far, odd, ham_blocks, block_counts, block_offsets, after):
    nblock, slots = ham_blocks.shape[:2]
    poles, _, _, width = near.shape
    reached = [i for i, (a, b) in enumerate(bounds) if a < REACH or b > nblock - REACH]
    outs, token = call(
        functools.partial(edge_kernel, nblock, [bounds[i] for i in reached]), "edge",
        [
            (block_counts, "smem"), (block_offsets, "smem"), (odd, "smem"), (ham_blocks, "hbm"),
            (near[None], "vmem"), (far[None], "vmem"),
        ]
        + [(slopes[i], "vmem") for i in reached],
        [(slopes[i].shape, F32, "vmem") for i in reached], after,
        scratch=[
            pltpu.VMEM((2 * REACH, slots, 2, width, width), F32),
            pltpu.VMEM((2 * width, poles * width), BF16),
            pltpu.VMEM((2 * width, poles * width), BF16),
            pltpu.VMEM((2 * width, poles * width), F32),
            pltpu.SemaphoreType.DMA((2 * REACH,)),
        ],
        limit=8,
    )
    slopes = list(slopes)
    for i, out in zip(reached, outs):
        slopes[i] = out
    return slopes, token


def finish_kernel(first, starts, chained, *refs):
    lead_ref, taken_ref, ghigh_ref, glow_ref, rho_ref, local_ref, received_ref = refs[:7]
    slope_refs = refs[7 : 7 + len(starts)]
    refs = refs[7 + len(starts) + (2 if chained else 0) :]
    out_ref, lead_out_ref, wide_ref, source_ref, panel_ref, sems = refs
    poles, _, _, width = slope_refs[0].shape
    rows = local_ref.shape[1]
    at = pl.ds(first, rows)
    lead_term = jnp.where(taken_ref[0] == 1, received_ref[...], local_ref[...])
    wide_ref[...] = lead_term
    copies = [pltpu.make_async_copy(wide_ref, lead_out_ref.at[:, at, :], sems.at[poles])]
    copies[0].start()
    half = rows // 2
    for part_no in range(2):
        begin = part_no * half
        here = pl.ds(begin, half)
        there = pl.ds(first + begin, half)
        for lead in range(2):
            columns = slice(lead * width, (lead + 1) * width)
            pair = jnp.concatenate(
                [rho_ref[part, there, columns] + 0.25 * wide_ref[part, here, columns] for part in range(2)],
                axis=1,
            )
            high, low = split_high_low(pair)
            source_ref[lead, here, :] = (
                dot(high, ghigh_ref[lead]) + dot(high, glow_ref[lead]) + dot(low, ghigh_ref[lead])
            )
        for pole in range(poles):
            lead = lead_ref[pole]
            for slope_ref, start in zip(slope_refs, starts):
                low_row = max(start, first + begin)
                high_row = min(start + slope_ref.shape[2], first + begin + half)
                if low_row >= high_row:
                    continue
                from_ = pl.ds(low_row - start, high_row - low_row)
                to = pl.ds(low_row - first, high_row - low_row)
                panel_ref[pole, 0, to, :] = slope_ref[pole, 0, from_, :] + source_ref[lead, to, width:]
                panel_ref[pole, 1, to, :] = slope_ref[pole, 1, from_, :] - source_ref[lead, to, :width]
            copies.append(
                pltpu.make_async_copy(
                    panel_ref.at[pole, :, here, :], out_ref.at[pole, :, there, :], sems.at[part_no * (poles + 1) + pole]
                )
            )
            copies[-1].start()
    for copy in copies:
        copy.wait()


def finish_rows(
    first, slopes, pieces, local, received, taken, rho_panel, ghigh, glow, pole_lead, results, out_shape, after, cost
):
    poles, _, _, width = out_shape
    rows = local.shape[1]
    starts = []
    touched = []
    for piece, (a, b) in zip(slopes, pieces):
        if a * width < first + rows and b * width > first:
            starts.append(a * width)
            touched.append((piece, "vmem"))
    operands = [
        (pole_lead, "smem"), (taken, "smem"), (ghigh, "vmem"), (glow, "vmem"), (rho_panel, "vmem"),
        (local, "vmem"), (received, "vmem"), *touched,
    ]
    aliases = None
    if results is not None:
        aliases = {len(operands) + i: i for i in range(2)}
        operands += [(result, "any") for result in results]
    return call(
        functools.partial(finish_kernel, first, starts, results is not None),
        "finish", operands,
        [(out_shape, F32, "any"), (rho_panel.shape, F32, "any")], after,
        scratch=[
            pltpu.VMEM((2, rows, 2 * width), F32),
            pltpu.VMEM((2, rows, 2 * width), F32),
            pltpu.VMEM((poles, 2, rows, width), F32),
            pltpu.SemaphoreType.DMA((2 * (poles + 1),)),
        ],
        aliases=aliases,
        cost=cost,
    )


def per_device(
    aux_modes,
    rho_panel,
    ham_blocks,
    block_counts,
    block_offsets,
    lead_gamma,
    pole_energy,
    residues,
    pole_lead,
):
    poles, _, rows, width = aux_modes.shape
    nblock = rows // width
    halo = REACH * width
    devices = lax.axis_size("row")
    odd = (lax.axis_index("row") % 2).astype(jnp.int32).reshape(1)
    count = lax.axis_size("pole")
    me = lax.axis_index("pole")
    inner = count // 2 - 1
    line = count % 2 == 0 and count >= 4

    taken = ((me == 0) | (me == count - 1)).astype(jnp.int32).reshape(1)

    sends = taken if line else jnp.ones_like(taken)

    chunks = CHUNKS
    ranges = [(c * rows // chunks, (c + 1) * rows // chunks) for c in range(chunks)]
    ranges = [ranges[1], ranges[0], *ranges[2:]]
    sizes = [b - a for a, b in ranges]

    (part,), token = call(
        functools.partial(first_kernel, *ranges[0], "pole" if line else None), "mix",
        [(pole_lead, "hbm"), (residues, "hbm"), (aux_modes, "hbm")],
        [((2, sizes[0], 2 * width), F32, "vmem")], [sends],
        scratch=[
            pltpu.VMEM((poles, 2, sizes[0], width), F32),
            pltpu.SMEM(pole_lead.shape, jnp.int32),
            pltpu.SMEM(residues.shape, F32),
            pltpu.SemaphoreType.DMA((4,)),
            pltpu.SemaphoreType.DMA((2,)),
        ],
    )
    later, token = call(
        functools.partial(later_kernel, ranges), "mix_later",
        [(pole_lead, "smem"), (residues, "smem"), (odd, "smem"), (lead_gamma, "vmem"), (aux_modes, "hbm")],
        [((2, size, 2 * width), F32, "vmem") for size in sizes]
        + [((poles, 2, halo, width), F32, "hbm")] * 2
        + [((2, 2 * width, 2 * width), BF16, "vmem")] * 2,
        [token],
        scratch=[
            pltpu.VMEM(aux_modes.shape, F32),
            pltpu.SemaphoreType.DMA((chunks,)),
            pltpu.SemaphoreType.DMA((2,)),
        ],
        limit=8,
    )
    near_edge, far_edge, ghigh, glow = later[chunks:]
    locals_ = later[:chunks]

    near_pairs = [(i, i + 1) for i in range(0, devices - 1, 2)]
    far_pairs = [(i, i + 1) for i in range(1, devices - 1, 2)]
    received = [None] * chunks

    def fold_pairs(stage):
        if stage < inner:
            return [(stage, stage + 1), (count - 1 - stage, count - 2 - stage)]
        if stage == inner:
            return [(inner, inner + 1), (inner + 1, inner)]
        j = 2 * inner + 1 - stage
        return [(j, j - 1), (count - 1 - j, count - j)]

    def send(c, stage):
        if line:
            mine = part if c == stage == 0 else locals_[c]
            received[c] = lax.ppermute(mine, "pole", fold_pairs(stage))
        else:
            received[c] = lax.psum(locals_[c], "pole")

    def take(c, stage):
        nonlocal token
        if stage <= inner:
            (locals_[c],), token = call(
                add_kernel, "add", [(locals_[c], "vmem"), (received[c], "vmem")],
                [(locals_[c].shape, F32, "vmem")], [token], cost=COSTS.get(("add", c, stage), 0),
            )
        else:
            j = 2 * inner + 1 - stage
            target = (me == j - 1) | (me == count - j)
            locals_[c] = jnp.where(target, received[c], locals_[c])

    slopes = [None] * 3
    results = None
    pieces = [(i * nblock // 3, (i + 1) * nblock // 3) for i in range(3)]
    near = far = None

    def work(piece):
        nonlocal token
        slopes[piece], token = ham_part(
            *pieces[piece], aux_modes, ham_blocks, block_counts, block_offsets, pole_energy,
            [token], COSTS.get(("ham", piece), 0),
        )

    def neighbours():
        nonlocal near, far, token
        (near, far), token = call(
            lambda: None, "pass", [], [], [token], through=[(near_edge, "hbm"), (far_edge, "hbm")],
            cost=COSTS.get(("pass",), 0),
        )
        near = lax.ppermute(near, "row", near_pairs + [(b, a) for a, b in near_pairs])
        far = lax.ppermute(far, "row", far_pairs + [(b, a) for a, b in far_pairs])

    def reach():
        nonlocal slopes, token
        slopes, token = edge_part(
            slopes, pieces, near, far, odd, ham_blocks, block_counts, block_offsets, [token]
        )

    def finish(c):
        nonlocal results, token
        local = locals_[c] if line else received[c]
        results, token = finish_rows(
            ranges[c][0], slopes, pieces, local, received[c], taken, rho_panel, ghigh, glow, pole_lead,
            results, aux_modes.shape, [token], COSTS.get(("finish", c), 0),
        )

    for c in range(chunks):
        send(c, 0)
    for step in make_plan(line, 2 * inner, len(pieces)):
        if step[0] == "ham":
            work(step[1])
        elif step[0] == "edge":
            reach()
        elif step[0] == "pass":
            neighbours()
        elif step[0] == "finish":
            finish(step[1])
        else:
            take(*step)
            send(step[0], step[1] + 1)
    return tuple(results)


def make_plan(line, stages, pieces):
    work = [("ham", i) for i in [1, 0, *range(2, pieces)]]
    ending = [("edge",)] + [("finish", c) for c in range(1, CHUNKS)]
    plan = [work.pop(0)]
    if not line:
        return plan + [("pass",)] + work + [("finish", 0)] + ending
    for turn in range(CHUNKS + stages - 1):
        for stage in range(stages):
            if 0 <= turn - stage < CHUNKS:
                plan.append((turn - stage, stage))
            if turn == stage == 0:
                plan.append(("pass",))
        if turn == CHUNKS - 1:
            plan.append(("finish", 0))
        if turn > 0 and work:
            plan.append(work.pop(0))
    return plan + work + ending


def solution(mesh):
    placed = (
        P(("grp", "pole"), None, "row", None),
        P(None, ("grp", "row"), None),
        P(("grp", "row"), None, None, None, None),
        P(("grp", "row")),
        P(("grp", "row"), None),
        P(),
        P(None, ("grp", "pole")),
        P(None, ("grp", "pole")),
        P(("grp", "pole")),
    )
    return jax.shard_map(
        per_device,
        mesh=mesh,
        in_specs=placed,
        out_specs=(P(("grp", "pole"), None, "row", None), P(None, ("grp", "row"), None)),
        check_vma=False,
    )
```
